128 devices in a mesh: clip: 16 (over z_lo, y, core), tile: 8 (over x, z_hi).
Axes of the slice: x: 4, y: 4, z: 4 (z_hi: 2, z_lo: 2; z = z_hi * 2 + z_lo), core: 2. Of those that a mesh axis runs over, the one named last changes fastest.
Arguments:
- features: bfloat16 [32, 128, 128, 256], P('clip', 'tile'), may hold values from -6 to 6
- conv_weight: bfloat16 [9, 256, 256], replicated, may hold values from -0.125 to 0.125
- codebook: bfloat16 [16384, 256], replicated, may hold values from -4 to 4
- codes: int32 [4, 32, 128, 128], P(None, 'clip', 'tile'), may hold values from 0 to 16383
- upstream: bfloat16 [32, 128, 128, 256], P('clip', 'tile'), may hold values from -6 to 6
Outputs:
- feature_grad: bfloat16 [32, 128, 128, 256], P('clip', 'tile')
- weight_grad: float32 [9, 256, 256], replicated
- codebook_grad: float32 [16384, 256], P(('clip', 'tile'))
The draws below stay inside these ranges and needn't reach their ends.
All inputs are finite; a program needn't handle non-finite values.
Results may differ from the reference program's by a relative error of at most 0.0085.
Values may be sent and summed in bfloat16 or wider, within the bound.
No kernel may reach another device: no remote copies, remote signals or barrier semaphores. Data moves between devices by JAX's collectives and lax.ppermute only.
A program may use at most 192 MiB of HBM per device.

```python
import jax
import jax.numpy as jnp
from jax import lax

C = 256
CODES = 16384
DEPTH = 4
W = 128
CLIPS = 32
H = 128


def with_ends(result, key, least, top_value):
    shape = result.shape
    index_at = [jax.random.randint(jax.random.fold_in(key, axis), (), 0, shape[axis]) for axis in range(len(shape))]
    result = result.at[tuple(index_at)].set(least)
    longest = shape.index(max(shape))
    index_at[longest] = (index_at[longest] + 1) % shape[longest]
    return result.at[tuple(index_at)].set(top_value)


def block_scale(own_key, dims, cuts, low, high):
    level, own = 1.0, jax.random.fold_in(own_key, 6)
    for dim, parts in cuts:
        draws = jnp.exp(jax.random.uniform(jax.random.fold_in(own, dim), (parts,), jnp.float32, low / len(cuts), high / len(cuts)))
        level = level * jnp.repeat(draws, dims[dim] // parts).reshape([-1 if axis == dim else 1 for axis in range(len(dims))])
    return level


def gaussian(stream_key, dims, spread, reach, shards=(), held_as=jnp.bfloat16):
    result = jax.random.normal(stream_key, dims, jnp.float32) * spread
    if len(shards) > 0:
        result = block_scale(stream_key, dims, shards, -0.22, 0.18) * result
    return jnp.clip(result, min=-reach, max=reach).astype(held_as)


def setup_inputs(seed: int = 0) -> dict:
    streams_of = jax.random.split(jax.random.key(seed), 6)
    return {
        "features": gaussian(streams_of[0], (CLIPS, H, W, C), 1.0, 6.0, ((0, 16), (1, 8))),
        "conv_weight": gaussian(streams_of[1], (9, C, C), (9 * C) ** -0.5, 0.125),
        "codebook": gaussian(streams_of[2], (CODES, C), 0.5, 4.0),
        "codes": with_ends(jax.random.randint(streams_of[3], (DEPTH, CLIPS, H, W), 0, CODES), jax.random.fold_in(streams_of[3], 1), 0, CODES - 1).astype(jnp.int32),
        "upstream": gaussian(streams_of[4], (CLIPS, H, W, C), 1.0, 6.0, ((0, 16), (1, 8))),
    }


BETA = 0.25


def clip_step(carry, inputs, weights, table):
    wsum, term = carry
    feats, cot, ids = inputs
    rows = feats.shape[0]
    width = feats.shape[1]
    padded = jnp.pad(feats.astype(jnp.float32), ((1, 1), (1, 1), (0, 0)))
    latent = jnp.zeros((rows, width, weights.shape[2]), jnp.float32)
    for a in range(3):
        for b in range(3):
            latent = latent + jnp.einsum("hwc,cd->hwd", padded[a:a + rows, b:b + width], weights[3 * a + b])
    resid = latent
    total = jnp.zeros_like(latent)
    stacked = []
    for depth in range(DEPTH):
        resid = resid - jnp.take(table, ids[depth], axis=0).astype(jnp.float32)
        total = total + resid
        stacked.append(resid)
    grad_bf = (cot.astype(jnp.float32) + 2.0 * BETA * total).astype(jnp.bfloat16)
    grad = grad_bf.astype(jnp.float32)
    gpad = jnp.pad(grad, ((1, 1), (1, 1), (0, 0)))
    back = jnp.zeros_like(latent)
    pieces = []
    for a in range(3):
        for b in range(3):
            back = back + jnp.einsum("hwd,cd->hwc", gpad[2 - a:2 - a + rows, 2 - b:2 - b + width], weights[3 * a + b])
            pieces.append(jnp.einsum("hwc,hwd->cd", padded[a:a + rows, b:b + width], grad))
    wsum = wsum + jnp.stack(pieces)
    values = -2.0 * jnp.stack(stacked).reshape(-1, latent.shape[2])
    term = term + jax.ops.segment_sum(values, ids.reshape(-1), num_segments=CODES)
    return (wsum, term), back.astype(jnp.bfloat16)


def reference(features, conv_weight, codebook, codes, upstream):
    weights = conv_weight.astype(jnp.float32)
    chans = features.shape[3]
    start = (jnp.zeros((9, chans, chans), jnp.float32), jnp.zeros((CODES, chans), jnp.float32))
    ids = jnp.moveaxis(codes, 0, 1)
    (wsum, term), back = lax.scan(lambda c, x: clip_step(c, x, weights, codebook), start, (features, upstream, ids))
    return back, wsum, term
```

```python
import jax
import jax.numpy as jnp
from jax import lax
from jax.experimental import pallas as pl
from jax.experimental.pallas import tpu as pltpu
from jax.sharding import PartitionSpec as P

BETA = 0.25
BOTH = ("clip", "tile")
F32, BF16 = jnp.float32, jnp.bfloat16

CHANS = 256
CODES = 16384
DEPTHS = 4
COLS = 128
ROWS = 16
HERE = 2
SPOTS = HERE * ROWS * COLS
BLOCK = 4 * COLS
BLOCKS = SPOTS // BLOCK
GROUP = 16
GROUPS = DEPTHS * SPOTS // GROUP
SPILL = 256
TABLE_STEP = 4096
TABLE_STEPS = CODES // TABLE_STEP
SHARE = CODES // 128
OUT_STEPS = 8
FIRST_OUT = TABLE_STEPS + BLOCKS


def lin(x, y, z, core):
    return (((z % 2) * 4 + y) * 2 + core) * 8 + x * 2 + z // 2


def moves(where):
    return [
        (lin(x, y, z, c), lin(*where(x, y, z, c)))
        for x in range(4)
        for y in range(4)
        for z in range(4)
        for c in range(2)
    ]


SWAP = moves(lambda x, y, z, c: (x, y, z, 1 - c))


def first_ring(d):
    return moves(lambda x, y, z, c: ((x + d) % 4, y, z, c) if c == 0 else (x, (y + d) % 4, z, c))


PLANES = [[lin(x, y, z, 0) for y in range(4) for z in range(4)] for x in range(4)] + [
    [lin(x, y, z, 1) for x in range(4) for z in range(4)] for y in range(4)
]


def place():
    clip, tile = lax.axis_index("clip"), lax.axis_index("tile")
    core, y, z_lo = clip % 2, (clip // 2) % 4, clip // 8
    x, z_hi = tile // 2, tile % 2
    return jnp.stack([x, y, z_hi * 2 + z_lo, core]).astype(jnp.int32)


def owner(x0, y0, core, j, m):
    other, z = m // 4, m % 4
    x = jnp.where(core == 0, (x0 + j) % 4, other)
    y = jnp.where(core == 0, other, (y0 + j) % 4)
    return lin(x, y, z, core)


def shifted(value, by):
    n = value.shape[0]
    col = lax.broadcasted_iota(jnp.int32, value.shape, 0) % COLS
    if by == 1:
        return jnp.where(col == 0, 0.0, pltpu.roll(value, 1, axis=0))
    return jnp.where(col == COLS - 1, 0.0, pltpu.roll(value, n - 1, axis=0))


def quantizer_kernel(
    codes, plain, spilled, info,
    table_in, feats, above, below, weights, up,
    grad, send, keep,
    table, sums, lat, window, sems,
):
    i = pl.program_id(0)

    def window_copies():
        found = []
        for n in range(HERE):
            for source, row, count in ((above, 0, 1), (feats, 1, ROWS), (below, ROWS + 1, 1)):
                found.append(
                    pltpu.make_async_copy(
                        source.at[n], window.at[n, pl.ds(row, count)], sems.at[len(found)]
                    )
                )
        return found

    @pl.when(i == 0)
    def _():
        for copy in window_copies():
            copy.start()

    @pl.when(i < TABLE_STEPS)
    def _():
        base = pl.multiple_of(i * (2 * TABLE_STEP), 8)

        def convert(t, carry):
            part = table_in[pl.ds(pl.multiple_of(t * 512, 16), 512), :].astype(F32)
            at = pl.multiple_of(base + t * 1024, 8)
            table[pl.ds(at, 512, stride=2), :] = part[:, :128]
            table[pl.ds(at + 1, 512, stride=2), :] = part[:, 128:]
            sums[pl.ds(at, 1024), :] = jnp.zeros((1024, 128), F32)
            return carry

        lax.fori_loop(0, TABLE_STEP // 512, convert, 0)

    @pl.when(i == TABLE_STEPS)
    def _():
        for copy in window_copies():
            copy.wait()
        sums[pl.ds(2 * CODES, 2 * SPILL), :] = jnp.zeros((2 * SPILL, 128), F32)

        def lend(s, carry):
            table[pl.ds(2 * (CODES + s), 2), :] = table[pl.ds(spilled[s], 2), :]
            return carry

        lax.fori_loop(0, jnp.minimum(info[4], SPILL), lend, 0)

    @pl.when((i >= TABLE_STEPS) & (i < FIRST_OUT))
    def _():
        block = i - TABLE_STEPS
        clip = block // (ROWS // 4)
        row = (block % (ROWS // 4)) * 4
        conv = None
        for a in range(3):
            part = window[clip, pl.ds(row + a, 4)].reshape(BLOCK, CHANS)
            term = jnp.dot(part, weights[a], preferred_element_type=F32)
            conv = term if conv is None else conv + term
        latent = (
            shifted(conv[:, :CHANS], 1)
            + conv[:, CHANS : 2 * CHANS]
            + shifted(conv[:, 2 * CHANS :], -1)
        )
        lat[pl.ds(0, BLOCK, stride=2), :] = latent[:, :128]
        lat[pl.ds(1, BLOCK, stride=2), :] = latent[:, 128:]

        def resids(at, ids):
            found = []
            for r in range(4):
                place_r = pl.ds(2 * (r * COLS + at), 2)
                resid, total = lat[place_r, :], None
                for d in range(DEPTHS):
                    k = ids(r, d)
                    resid = resid - table[pl.ds(k, 2), :]
                    total = resid if total is None else total + resid
                    found.append((k, resid))
                lat[place_r, :] = total
            return found

        def step(at, carry):
            base = (block * COLS + at) * GROUP
            found = resids(at, lambda r, d: codes[base + (r * DEPTHS + d)])
            new = [sums[pl.ds(k, 2), :] + v for k, v in found]
            for (k, _), v in zip(found, new):
                sums[pl.ds(k, 2), :] = v
            return carry

        def slow_step(at, carry):
            base = (block * COLS + at) * GROUP
            for k, v in resids(at, lambda r, d: plain[base + (r * DEPTHS + d)]):
                sums[pl.ds(k, 2), :] = sums[pl.ds(k, 2), :] + v
            return carry

        @pl.when(info[4] <= SPILL)
        def _():
            lax.fori_loop(0, COLS, step, 0, unroll=2)

        @pl.when(info[4] > SPILL)
        def _():
            lax.fori_loop(0, COLS, slow_step, 0)

        total = jnp.concatenate(
            [lat[pl.ds(0, BLOCK, stride=2), :], lat[pl.ds(1, BLOCK, stride=2), :]], axis=1
        )
        grad[...] = (up[...].astype(F32) + 2.0 * BETA * total).astype(BF16)

    @pl.when((i == FIRST_OUT) & (info[4] <= SPILL))
    def _():
        def give_back(s, carry):
            k = spilled[s]
            sums[pl.ds(k, 2), :] = sums[pl.ds(k, 2), :] + sums[pl.ds(2 * (CODES + s), 2), :]
            return carry

        lax.fori_loop(0, info[4], give_back, 0)

    def put_out(out, core, j):
        for m in range(16):
            at = pl.multiple_of(owner(info[0], info[1], core, j, m) * (2 * SHARE), 8)
            out[0, m, :, :128] = (sums[pl.ds(at, SHARE, stride=2), :] * -2.0).astype(BF16)
            out[0, m, :, 128:] = (sums[pl.ds(at + 1, SHARE, stride=2), :] * -2.0).astype(BF16)

    @pl.when((i >= FIRST_OUT) & (i < FIRST_OUT + 4))
    def _():
        put_out(send, 1 - info[3], i - FIRST_OUT)

    @pl.when(i >= FIRST_OUT + 4)
    def _():
        put_out(keep, info[3], i - FIRST_OUT - 4)


def quantizer(codes, plain, spilled, info, codebook, feats, above, below, weights, up):
    def spot(i, *_):
        return (jnp.clip(i - TABLE_STEPS, 0, BLOCKS - 1), 0)

    out_block = (1, 16, SHARE, CHANS)
    return pl.pallas_call(
        quantizer_kernel,
        grid_spec=pltpu.PrefetchScalarGridSpec(
            num_scalar_prefetch=4,
            grid=(FIRST_OUT + OUT_STEPS,),
            in_specs=[
                pl.BlockSpec(
                    (TABLE_STEP, CHANS), lambda i, *_: (jnp.minimum(i, TABLE_STEPS - 1), 0)
                ),
                pl.BlockSpec(memory_space=pl.ANY),
                pl.BlockSpec(memory_space=pl.ANY),
                pl.BlockSpec(memory_space=pl.ANY),
                pl.BlockSpec((3, CHANS, 3 * CHANS), lambda i, *_: (0, 0, 0)),
                pl.BlockSpec((BLOCK, CHANS), spot),
            ],
            out_specs=[
                pl.BlockSpec((BLOCK, CHANS), spot),
                pl.BlockSpec(out_block, lambda i, *_: (jnp.clip(i - FIRST_OUT, 0, 3), 0, 0, 0)),
                pl.BlockSpec(
                    out_block, lambda i, *_: (jnp.clip(i - FIRST_OUT - 4, 0, 3), 0, 0, 0)
                ),
            ],
            scratch_shapes=[
                pltpu.VMEM((2 * (CODES + SPILL), 128), F32),
                pltpu.VMEM((2 * (CODES + SPILL), 128), F32),
                pltpu.VMEM((2 * BLOCK, 128), F32),
                pltpu.VMEM((HERE, ROWS + 2, COLS, CHANS), BF16),
                pltpu.SemaphoreType.DMA((3 * HERE,)),
            ],
        ),
        out_shape=[
            jax.ShapeDtypeStruct((SPOTS, CHANS), BF16),
            jax.ShapeDtypeStruct((4, 16, SHARE, CHANS), BF16),
            jax.ShapeDtypeStruct((4, 16, SHARE, CHANS), BF16),
        ],
        compiler_params=pltpu.CompilerParams(
            vmem_limit_bytes=58 << 20, dimension_semantics=("arbitrary",)
        ),
        cost_estimate=pl.CostEstimate(
            flops=2 * 9 * SPOTS * CHANS * CHANS, bytes_accessed=32 << 20, transcendentals=0
        ),
    )(codes, plain, spilled, info, codebook, feats, above, below, weights, up)


def weight_kernel(info, feats, above, below, grad, send, keep, window, total, sems):
    i = pl.program_id(0)

    def window_copies():
        found = []
        for n in range(HERE):
            for source, row, count in ((above, 0, 1), (feats, 1, ROWS), (below, ROWS + 1, 1)):
                found.append(
                    pltpu.make_async_copy(
                        source.at[n], window.at[n, pl.ds(row, count)], sems.at[len(found)]
                    )
                )
        return found

    @pl.when(i == 0)
    def _():
        for copy in window_copies():
            copy.start()
        for copy in window_copies():
            copy.wait()

    clip = i // (ROWS // 4)
    row = (i % (ROWS // 4)) * 4
    mid = grad[...].astype(F32)
    wide = jnp.concatenate(
        [shifted(mid, -1).astype(BF16), grad[...], shifted(mid, 1).astype(BF16)], axis=1
    )
    for a in range(3):
        part = window[clip, pl.ds(row + a, 4)].reshape(BLOCK, CHANS)
        term = lax.dot_general(part, wide, (((0,), (0,)), ((), ())), preferred_element_type=F32)

        @pl.when(i == 0)
        def _():
            total[pl.ds(a * CHANS, CHANS), :] = term

        @pl.when(i > 0)
        def _():
            total[pl.ds(a * CHANS, CHANS), :] += term

    @pl.when(i == BLOCKS - 1)
    def _():
        for out, core in ((send, 1 - info[3]), (keep, info[3])):
            for j in range(4):
                for m in range(16):
                    b = jnp.minimum(owner(info[0], info[1], core, j, m), 95)
                    rows = total[pl.ds(pl.multiple_of(b * 8, 8), 8), :]
                    for q in range(3):
                        out[j, m, pl.ds(8 * q, 8), :] = rows[:, q * CHANS : (q + 1) * CHANS]


def weight_sums(info, feats, above, below, grad):
    shape = (4, 16, 24, CHANS)
    return pl.pallas_call(
        weight_kernel,
        grid_spec=pltpu.PrefetchScalarGridSpec(
            num_scalar_prefetch=1,
            grid=(BLOCKS,),
            in_specs=[
                pl.BlockSpec(memory_space=pl.ANY),
                pl.BlockSpec(memory_space=pl.ANY),
                pl.BlockSpec(memory_space=pl.ANY),
                pl.BlockSpec((BLOCK, CHANS), lambda i, *_: (i, 0)),
            ],
            out_specs=[
                pl.BlockSpec(shape, lambda i, *_: (0, 0, 0, 0)),
                pl.BlockSpec(shape, lambda i, *_: (0, 0, 0, 0)),
            ],
            scratch_shapes=[
                pltpu.VMEM((HERE, ROWS + 2, COLS, CHANS), BF16),
                pltpu.VMEM((3 * CHANS, 3 * CHANS), F32),
                pltpu.SemaphoreType.DMA((3 * HERE,)),
            ],
        ),
        out_shape=[jax.ShapeDtypeStruct(shape, F32)] * 2,
        compiler_params=pltpu.CompilerParams(
            vmem_limit_bytes=32 << 20, dimension_semantics=("arbitrary",)
        ),
        cost_estimate=pl.CostEstimate(
            flops=2 * 9 * SPOTS * CHANS * CHANS, bytes_accessed=8 << 20, transcendentals=0
        ),
    )(info, feats, above, below, grad)


def back_kernel(grad, above, below, weights, out, window, sems):
    i = pl.program_id(0)

    def window_copies():
        found = []
        for n in range(HERE):
            for source, row, count in ((above, 0, 1), (grad, 1, ROWS), (below, ROWS + 1, 1)):
                found.append(
                    pltpu.make_async_copy(
                        source.at[n], window.at[n, pl.ds(row, count)], sems.at[len(found)]
                    )
                )
        return found

    @pl.when(i == 0)
    def _():
        for copy in window_copies():
            copy.start()
        for copy in window_copies():
            copy.wait()

    clip = i // (ROWS // 4)
    row = (i % (ROWS // 4)) * 4
    conv = None
    for a in range(3):
        part = window[clip, pl.ds(row + 2 - a, 4)].reshape(BLOCK, CHANS)
        term = jnp.dot(part, weights[a], preferred_element_type=F32)
        conv = term if conv is None else conv + term
    back = (
        shifted(conv[:, :CHANS], -1)
        + conv[:, CHANS : 2 * CHANS]
        + shifted(conv[:, 2 * CHANS :], 1)
    )
    out[...] = back.astype(BF16)


def feature_grads(grad, above, below, weights):
    return pl.pallas_call(
        back_kernel,
        grid=(BLOCKS,),
        in_specs=[
            pl.BlockSpec(memory_space=pl.ANY),
            pl.BlockSpec(memory_space=pl.ANY),
            pl.BlockSpec(memory_space=pl.ANY),
            pl.BlockSpec((3, CHANS, 3 * CHANS), lambda i: (0, 0, 0)),
        ],
        out_specs=pl.BlockSpec((BLOCK, CHANS), lambda i: (i, 0)),
        scratch_shapes=[
            pltpu.VMEM((HERE, ROWS + 2, COLS, CHANS), BF16),
            pltpu.SemaphoreType.DMA((3 * HERE,)),
        ],
        out_shape=jax.ShapeDtypeStruct((SPOTS, CHANS), BF16),
        compiler_params=pltpu.CompilerParams(
            vmem_limit_bytes=32 << 20, dimension_semantics=("arbitrary",)
        ),
        cost_estimate=pl.CostEstimate(
            flops=2 * 9 * SPOTS * CHANS * CHANS, bytes_accessed=8 << 20, transcendentals=0
        ),
    )(grad, above, below, weights)


def edges(array):
    n = lax.axis_size("tile")
    up = [(i, i + 1) for i in range(n - 1)]
    down = [(i + 1, i) for i in range(n - 1)]
    above = lax.ppermute(array[:, -1:], "tile", up)
    below = lax.ppermute(array[:, :1], "tile", down)
    return above, below


def entry_lists(codes):
    parts = codes.reshape(DEPTHS, BLOCKS, 4, COLS)
    cells = [parts[d, :, r] for r in range(4) for d in range(DEPTHS)]
    later = []
    for a in range(GROUP):
        hit = jnp.zeros((BLOCKS, COLS), jnp.bool_)
        for b in range(a + 1, GROUP):
            hit = hit | (cells[a] == cells[b])
        later.append(hit)
    flags = jnp.stack(later).reshape(128, 128).astype(F32)
    entries = jnp.stack(cells).reshape(128, 128)
    lane = jnp.arange(128)
    inside = jnp.dot(flags, (lane[:, None] < lane[None, :]).astype(F32))
    per_row = flags.sum(1)
    ahead = jnp.where(lane[None, :] < lane[:, None], per_row[None, :], 0.0).sum(1)
    rank = (inside + ahead[:, None]).astype(jnp.int32)
    total = per_row.sum().astype(jnp.int32)
    hits = flags > 0
    marked = jnp.where(hits, CODES + rank, entries)
    wanted = jnp.where(hits, rank, -1).reshape(1, -1) == jnp.arange(SPILL)[:, None]
    spilled = jnp.where(wanted, entries.reshape(1, -1), 0).sum(1)

    def grouped(array):
        return (2 * array).reshape(GROUP, GROUPS).T.reshape(-1)

    return grouped(marked), grouped(entries), 2 * spilled, total


def on_device(features, conv_weight, codebook, codes, upstream):
    info = place()
    above, below = edges(features)
    taps = conv_weight.reshape(3, 3, CHANS, CHANS)
    forward = taps.transpose(0, 2, 1, 3).reshape(3, CHANS, 3 * CHANS)
    backward = taps.transpose(0, 3, 1, 2).reshape(3, CHANS, 3 * CHANS)
    marked, plain, spilled, total = entry_lists(codes)
    info = jnp.concatenate([info, total[None]])
    grad, send, keep = quantizer(
        marked, plain, spilled, info, codebook, features, above, below, forward,
        upstream.reshape(SPOTS, CHANS),
    )
    got = lax.ppermute(send, BOTH, SWAP)
    weight_send, weight_keep = weight_sums(info, features, above, below, grad)
    weight_got = lax.ppermute(weight_send.astype(BF16), BOTH, SWAP)
    grad4 = grad.reshape(features.shape)
    back = feature_grads(grad4, *edges(grad4), backward)
    chip = jnp.concatenate(
        [
            (keep.astype(F32) + got.astype(F32)).astype(BF16),
            (weight_keep + weight_got.astype(F32)).astype(BF16),
        ],
        axis=2,
    )
    ring = chip[0].astype(F32)
    for d in (1, 2, 3):
        ring = ring + lax.ppermute(chip[d], BOTH, first_ring(d)).astype(F32)
    plane = lax.all_to_all(ring.astype(BF16), BOTH, 0, 0, axis_index_groups=PLANES)
    block = plane.astype(F32).sum(0)
    code_part = block[:SHARE]
    piece = block[SHARE:].astype(BF16)
    pieces = lax.all_to_all(jnp.broadcast_to(piece[None], (128, 24, CHANS)), BOTH, 0, 0)
    weight_grad = pieces[:96].reshape(96, 3, 8, CHANS).transpose(0, 2, 1, 3)
    weight_grad = weight_grad.reshape(3, CHANS, 3, CHANS).transpose(0, 2, 1, 3)
    weight_grad = weight_grad.reshape(9, CHANS, CHANS).astype(F32)
    return back.reshape(features.shape), weight_grad, code_part


def solution(mesh):
    in_specs = (
        P("clip", "tile", None, None),
        P(),
        P(),
        P(None, "clip", "tile", None),
        P("clip", "tile", None, None),
    )
    out_specs = (P("clip", "tile", None, None), P(), P(BOTH, None))
    return jax.shard_map(
        on_device, mesh=mesh, in_specs=in_specs, out_specs=out_specs, check_vma=False
    )
```

```python
import functools

import jax
import jax.numpy as jnp
from jax import lax
from jax.experimental import pallas as pl
from jax.experimental.pallas import tpu as pltpu
from jax.sharding import PartitionSpec as P

BETA = 0.25
BOTH = ("clip", "tile")
F32, BF16 = jnp.float32, jnp.bfloat16

CHANS = 256
CODES = 16384
DEPTHS = 4
COLS = 128
ROWS = 16
HERE = 2
SPOTS = HERE * ROWS * COLS
BLOCK = 4 * COLS
BLOCKS = SPOTS // BLOCK
GROUP = 16
GROUPS = DEPTHS * SPOTS // GROUP
SPILL = 64
CHUNKS = 8
UNROLL = 8
SHARE = CODES // 128


def lin(x, y, z, core):
    return (((z % 2) * 4 + y) * 2 + core) * 8 + x * 2 + z // 2


def moves(where):
    return [
        (lin(x, y, z, c), lin(*where(x, y, z, c)))
        for x in range(4)
        for y in range(4)
        for z in range(4)
        for c in range(2)
    ]


SWAP = moves(lambda x, y, z, c: (x, y, z, 1 - c))


def first_ring(d):
    return moves(lambda x, y, z, c: ((x + d) % 4, y, z, c) if c == 0 else (x, (y + d) % 4, z, c))


PLANES = [[lin(x, y, z, 0) for y in range(4) for z in range(4)] for x in range(4)] + [
    [lin(x, y, z, 1) for x in range(4) for z in range(4)] for y in range(4)
]


def place():
    clip, tile = lax.axis_index("clip"), lax.axis_index("tile")
    core, y, z_lo = clip % 2, (clip // 2) % 4, clip // 8
    x, z_hi = tile // 2, tile % 2
    return jnp.stack([x, y, z_hi * 2 + z_lo, core]).astype(jnp.int32)


def owner(x0, y0, core, j, m):
    other, z = m // 4, m % 4
    x = jnp.where(core == 0, (x0 + j) % 4, other)
    y = jnp.where(core == 0, other, (y0 + j) % 4)
    return lin(x, y, z, core)


def shifted(value, by):
    n = value.shape[0]
    col = lax.broadcasted_iota(jnp.int32, value.shape, 0) % COLS
    if by == 1:
        return jnp.where(col == 0, 0.0, pltpu.roll(value, 1, axis=0))
    return jnp.where(col == COLS - 1, 0.0, pltpu.roll(value, n - 1, axis=0))


def window_copies(above, mid, below, window, sems, first=0):
    found = []
    for n in range(HERE):
        for source, row, count in ((above, 0, 1), (mid, 1, ROWS), (below, ROWS + 1, 1)):
            found.append(
                pltpu.make_async_copy(
                    source.at[n], window.at[n, pl.ds(row, count)], sems.at[first + len(found)]
                )
            )
    return found


def list_kernel(codes, marked, spilled, count):
    cells = [codes[pl.ds(d * 32 + r, BLOCKS, stride=4), :] for r in range(4) for d in range(DEPTHS)]
    later = []
    for a in range(GROUP):
        hit = None
        for b in range(a + 1, GROUP):
            same = (cells[a] == cells[b]).astype(jnp.int32)
            hit = same if hit is None else jnp.maximum(hit, same)
        later.append(jnp.zeros_like(cells[a]) if hit is None else hit)
    flags = jnp.concatenate(later, axis=0)
    entries = jnp.concatenate(cells, axis=0)
    line = lax.broadcasted_iota(jnp.int32, (128, 128), 0)
    lane = lax.broadcasted_iota(jnp.int32, (128, 128), 1)
    bits = flags.astype(F32)
    inside = jnp.dot(bits, (line < lane).astype(F32), preferred_element_type=F32)
    per_row = jnp.dot(bits, jnp.ones((128, 128), F32), preferred_element_type=F32)
    ahead = jnp.dot((lane < line).astype(F32), per_row, preferred_element_type=F32)
    rank = (inside + ahead).astype(jnp.int32)
    marked[...] = 2 * jnp.where(flags > 0, CODES + rank, entries)
    rank = jnp.where(flags > 0, rank, -1)
    for s in range(SPILL):
        spilled[pl.ds(s, 1), :] = jnp.sum(
            jnp.where(rank == s, 2 * entries, 0), axis=0, keepdims=True
        )
    spilled[...] = jnp.broadcast_to(
        jnp.sum(spilled[...].astype(F32), axis=1, keepdims=True), (SPILL, 128)
    ).astype(jnp.int32)
    whole = jnp.sum(per_row, axis=0, keepdims=True).astype(jnp.int32)
    count[...] = jnp.broadcast_to(whole, (8, 128))


def entry_lists(codes):
    ints = jnp.int32
    return pl.pallas_call(
        list_kernel,
        out_shape=[
            jax.ShapeDtypeStruct((128, 128), ints),
            jax.ShapeDtypeStruct((SPILL, 128), ints),
            jax.ShapeDtypeStruct((8, 128), ints),
        ],
    )(codes.reshape(128, 128))


def quantizer_kernel(
    spilled, info, count,
    marked, plain, codebook, feats, above, below, weights, up,
    grad, send, keep,
    table, sums, lat, raw, near, taps, window, ids, sems,
):
    many = count[0, 0]
    windows = window_copies(above, feats, below, window, sems)
    get_taps = pltpu.make_async_copy(weights, taps, sems.at[6])
    get_ids = pltpu.make_async_copy(marked, ids, sems.at[7])
    get_up = pltpu.make_async_copy(up, near, sems.at[8])
    chunk = CODES // CHUNKS

    def get_table(c):
        rows = pl.ds(c * chunk, chunk)
        return pltpu.make_async_copy(codebook.at[rows], raw.at[rows], sems.at[16 + c])

    for copy in windows + [get_taps]:
        copy.start()
    for c in range(CHUNKS):
        get_table(c).start()
    get_ids.start()
    get_up.start()
    for copy in windows + [get_taps]:
        copy.wait()

    def convolve(block, carry):
        clip = block // (ROWS // 4)
        row = (block % (ROWS // 4)) * 4
        cols = [None] * 3
        for a in range(3):
            part = window[clip, pl.ds(row + a, 4)].reshape(BLOCK, CHANS)
            for b in range(3):
                term = jnp.dot(part, taps[3 * a + b], preferred_element_type=F32)
                cols[b] = term if a == 0 else cols[b] + term
        latent = shifted(cols[0], 1) + cols[1] + shifted(cols[2], -1)
        at = pl.multiple_of(block * (2 * BLOCK), 8)
        lat[pl.ds(at, BLOCK, stride=2), :] = latent[:, :128]
        lat[pl.ds(at + 1, BLOCK, stride=2), :] = latent[:, 128:]
        return carry

    lax.fori_loop(0, BLOCKS, convolve, 0)

    for c in range(CHUNKS):
        get_table(c).wait()

        def convert(t, carry):
            at = pl.multiple_of(c * chunk + t * 512, 16)
            part = raw[pl.ds(at, 512), :].astype(F32)
            at = pl.multiple_of(2 * at, 8)
            table[pl.ds(at, 512, stride=2), :] = part[:, :128]
            table[pl.ds(at + 1, 512, stride=2), :] = part[:, 128:]
            sums[pl.ds(at, 1024), :] = jnp.zeros((1024, 128), F32)
            return carry

        lax.fori_loop(0, chunk // 512, convert, 0)

    sums[pl.ds(2 * CODES, 2 * SPILL), :] = jnp.zeros((2 * SPILL, 128), F32)

    def lend(s, carry):
        table[pl.ds(2 * (CODES + s), 2), :] = table[pl.ds(spilled[s, 0], 2), :]
        return carry

    lax.fori_loop(0, jnp.minimum(many, SPILL), lend, 0)

    def resids(spot, code):
        found = []
        for r in range(4):
            here = pl.ds(2 * (spot + r * COLS), 2)
            resid, total = lat[here, :], None
            for d in range(DEPTHS):
                k = code(r, d)
                resid = resid - table[pl.ds(k, 2), :]
                total = resid if total is None else total + resid
                found.append((k, resid))
            lat[here, :] = total
        return found

    get_ids.wait()

    @pl.when(many <= SPILL)
    def _():
        def blocks(block, carry):
            def step(col, carry):
                first = block * COLS + col
                found = resids(
                    block * BLOCK + col, lambda r, d: ids[first + (r * DEPTHS + d) * (GROUPS)]
                )
                new = [sums[pl.ds(k, 2), :] + v for k, v in found]
                for (k, _), v in zip(found, new):
                    sums[pl.ds(k, 2), :] = v
                return carry

            return lax.fori_loop(0, COLS, step, carry, unroll=UNROLL)

        lax.fori_loop(0, BLOCKS, blocks, 0)

        def give_back(s, carry):
            k = spilled[s, 0]
            sums[pl.ds(k, 2), :] = sums[pl.ds(k, 2), :] + sums[pl.ds(2 * (CODES + s), 2), :]
            return carry

        lax.fori_loop(0, many, give_back, 0)

    @pl.when(many > SPILL)
    def _():
        again = pltpu.make_async_copy(plain, ids, sems.at[7])
        again.start()
        again.wait()

        def blocks(block, carry):
            def step(col, carry):
                spot = block * BLOCK + col
                for k, v in resids(spot, lambda r, d: 2 * ids[d * SPOTS + spot + r * COLS]):
                    sums[pl.ds(k, 2), :] = sums[pl.ds(k, 2), :] + v
                return carry

            return lax.fori_loop(0, COLS, step, carry)

        lax.fori_loop(0, BLOCKS, blocks, 0)

    get_up.wait()

    def put_grad(block):
        rows = pl.ds(pl.multiple_of(block * BLOCK, 16), BLOCK)
        return pltpu.make_async_copy(near.at[rows], grad.at[rows], sems.at[8 + block])

    def gradient(block, carry):
        rows = pl.ds(pl.multiple_of(block * BLOCK, 16), BLOCK)
        at = pl.multiple_of(block * (2 * BLOCK), 8)
        total = jnp.concatenate(
            [lat[pl.ds(at, BLOCK, stride=2), :], lat[pl.ds(at + 1, BLOCK, stride=2), :]], axis=1
        )
        near[rows, :] = (near[rows, :].astype(F32) + 2.0 * BETA * total).astype(BF16)
        put_grad(block).start()
        return carry

    lax.fori_loop(0, BLOCKS, gradient, 0)

    def put_out(out, first, j):
        rows = pl.ds((first + j) * 16 * SHARE, 16 * SHARE)
        return pltpu.make_async_copy(raw.at[rows], out.at[j], sems.at[16 + first + j])

    def fill(m, carry, first, core, j):
        at = pl.multiple_of(owner(info[0], info[1], core, j, m) * (2 * SHARE), 8)
        rows = pl.ds(pl.multiple_of(((first + j) * 16 + m) * SHARE, 16), SHARE)
        raw[rows, :128] = (sums[pl.ds(at, SHARE, stride=2), :] * -2.0).astype(BF16)
        raw[rows, 128:] = (sums[pl.ds(at + 1, SHARE, stride=2), :] * -2.0).astype(BF16)
        return carry

    for first, core, out in ((0, 1 - info[3], send), (4, info[3], keep)):
        for j in range(4):
            lax.fori_loop(0, 16, functools.partial(fill, first=first, core=core, j=j), 0, unroll=2)
            put_out(out, first, j).start()
    for block in range(BLOCKS):
        put_grad(block).wait()
    for first, out in ((0, send), (4, keep)):
        for j in range(4):
            put_out(out, first, j).wait()


def quantizer(marked, plain, spilled, info, count, codebook, feats, above, below, weights, up):
    hbm = pl.BlockSpec(memory_space=pl.ANY)
    smem = pl.BlockSpec(memory_space=pltpu.SMEM)
    out_shape = (4, 16 * SHARE, CHANS)
    return pl.pallas_call(
        quantizer_kernel,
        in_specs=[smem] * 3 + [hbm] * 8,
        out_specs=[hbm] * 3,
        scratch_shapes=[
            pltpu.VMEM((2 * (CODES + SPILL), 128), F32),
            pltpu.VMEM((2 * (CODES + SPILL), 128), F32),
            pltpu.VMEM((2 * SPOTS, 128), F32),
            pltpu.VMEM((CODES, CHANS), BF16),
            pltpu.VMEM((SPOTS, CHANS), BF16),
            pltpu.VMEM((9, CHANS, CHANS), BF16),
            pltpu.VMEM((HERE, ROWS + 2, COLS, CHANS), BF16),
            pltpu.SMEM((DEPTHS * SPOTS,), jnp.int32),
            pltpu.SemaphoreType.DMA((24,)),
        ],
        out_shape=[
            jax.ShapeDtypeStruct((SPOTS, CHANS), BF16),
            jax.ShapeDtypeStruct(out_shape, BF16),
            jax.ShapeDtypeStruct(out_shape, BF16),
        ],
        compiler_params=pltpu.CompilerParams(vmem_limit_bytes=58 << 20),
        cost_estimate=pl.CostEstimate(
            flops=2 * 9 * SPOTS * CHANS * CHANS, bytes_accessed=32 << 20, transcendentals=0
        ),
    )(spilled, info, count, marked, plain, codebook, feats, above, below, weights, up)


def weight_kernel(info, feats, above, below, grad, send, keep, window, total, sems):
    i = pl.program_id(0)

    copies = window_copies(above, feats, below, window, sems)

    @pl.when(i == 0)
    def _():
        for copy in copies:
            copy.start()
        for copy in copies:
            copy.wait()

    clip = i // (ROWS // 4)
    row = (i % (ROWS // 4)) * 4
    mid = grad[...].astype(F32)
    wide = jnp.concatenate(
        [shifted(mid, -1).astype(BF16), grad[...], shifted(mid, 1).astype(BF16)], axis=1
    )
    for a in range(3):
        part = window[clip, pl.ds(row + a, 4)].reshape(BLOCK, CHANS)
        term = lax.dot_general(part, wide, (((0,), (0,)), ((), ())), preferred_element_type=F32)

        @pl.when(i == 0)
        def _():
            total[pl.ds(a * CHANS, CHANS), :] = term

        @pl.when(i > 0)
        def _():
            total[pl.ds(a * CHANS, CHANS), :] += term

    @pl.when(i == BLOCKS - 1)
    def _():
        for out, core in ((send, 1 - info[3]), (keep, info[3])):
            for j in range(4):
                for m in range(16):
                    near = jnp.where(core == 0, info[0], info[1])
                    b = jnp.minimum(core * 64 + (near + j) % 4 * 16 + m, 95)
                    rows = total[pl.ds(pl.multiple_of(b * 8, 8), 8), :]
                    for q in range(3):
                        out[j, m, pl.ds(8 * q, 8), :] = rows[:, q * CHANS : (q + 1) * CHANS]


def weight_sums(info, feats, above, below, grad):
    shape = (4, 16, 24, CHANS)
    return pl.pallas_call(
        weight_kernel,
        grid_spec=pltpu.PrefetchScalarGridSpec(
            num_scalar_prefetch=1,
            grid=(BLOCKS,),
            in_specs=[
                pl.BlockSpec(memory_space=pl.ANY),
                pl.BlockSpec(memory_space=pl.ANY),
                pl.BlockSpec(memory_space=pl.ANY),
                pl.BlockSpec((BLOCK, CHANS), lambda i, *_: (i, 0)),
            ],
            out_specs=[
                pl.BlockSpec(shape, lambda i, *_: (0, 0, 0, 0)),
                pl.BlockSpec(shape, lambda i, *_: (0, 0, 0, 0)),
            ],
            scratch_shapes=[
                pltpu.VMEM((HERE, ROWS + 2, COLS, CHANS), BF16),
                pltpu.VMEM((3 * CHANS, 3 * CHANS), F32),
                pltpu.SemaphoreType.DMA((3 * HERE,)),
            ],
        ),
        out_shape=[jax.ShapeDtypeStruct(shape, F32)] * 2,
        compiler_params=pltpu.CompilerParams(
            vmem_limit_bytes=32 << 20, dimension_semantics=("arbitrary",)
        ),
        cost_estimate=pl.CostEstimate(
            flops=2 * 9 * SPOTS * CHANS * CHANS, bytes_accessed=8 << 20, transcendentals=0
        ),
    )(info, feats, above, below, grad)


def back_kernel(grad, above, below, weights, out, window, sems):
    i = pl.program_id(0)

    copies = window_copies(above, grad, below, window, sems)

    @pl.when(i == 0)
    def _():
        for copy in copies:
            copy.start()
        for copy in copies:
            copy.wait()

    clip = i // (ROWS // 4)
    row = (i % (ROWS // 4)) * 4
    cols = [None] * 3
    for a in range(3):
        part = window[clip, pl.ds(row + 2 - a, 4)].reshape(BLOCK, CHANS)
        for b in range(3):
            term = lax.dot_general(
                part, weights[3 * a + b], (((1,), (1,)), ((), ())), preferred_element_type=F32
            )
            cols[b] = term if a == 0 else cols[b] + term
    back = shifted(cols[0], -1) + cols[1] + shifted(cols[2], 1)
    out[...] = back.astype(BF16)


def feature_grads(grad, above, below, weights):
    return pl.pallas_call(
        back_kernel,
        grid=(BLOCKS,),
        in_specs=[
            pl.BlockSpec(memory_space=pl.ANY),
            pl.BlockSpec(memory_space=pl.ANY),
            pl.BlockSpec(memory_space=pl.ANY),
            pl.BlockSpec((9, CHANS, CHANS), lambda i: (0, 0, 0)),
        ],
        out_specs=pl.BlockSpec((BLOCK, CHANS), lambda i: (i, 0)),
        scratch_shapes=[
            pltpu.VMEM((HERE, ROWS + 2, COLS, CHANS), BF16),
            pltpu.SemaphoreType.DMA((3 * HERE,)),
        ],
        out_shape=jax.ShapeDtypeStruct((SPOTS, CHANS), BF16),
        compiler_params=pltpu.CompilerParams(
            vmem_limit_bytes=32 << 20, dimension_semantics=("arbitrary",)
        ),
        cost_estimate=pl.CostEstimate(
            flops=2 * 9 * SPOTS * CHANS * CHANS, bytes_accessed=8 << 20, transcendentals=0
        ),
    )(grad, above, below, weights)


def edges(array):
    n = lax.axis_size("tile")
    up = [(i, i + 1) for i in range(n - 1)]
    down = [(i + 1, i) for i in range(n - 1)]
    above = lax.ppermute(array[:, -1:], "tile", up)
    below = lax.ppermute(array[:, :1], "tile", down)
    return above, below


def on_device(features, conv_weight, codebook, codes, upstream):
    info = place()
    above, below = edges(features)
    marked, spilled, count = entry_lists(codes)
    grad, send, keep = quantizer(
        marked.reshape(-1), codes.reshape(-1), spilled, info, count, codebook, features, above,
        below, conv_weight, upstream.reshape(SPOTS, CHANS),
    )
    got = lax.ppermute(send, BOTH, SWAP)
    grad4 = grad.reshape(features.shape)
    grad_above, grad_below = edges(grad4)
    weight_send, weight_keep = weight_sums(info, features, above, below, grad)
    weight_got = lax.ppermute(weight_send.astype(BF16), BOTH, SWAP)
    weight_chip = (weight_keep + weight_got.astype(F32)).astype(BF16)
    keep, got, grad_above, grad_below, weight_chip = lax.optimization_barrier(
        (keep, got, grad_above, grad_below, weight_chip)
    )
    weight_ring = weight_chip[0].astype(F32)
    for d in (1, 2, 3):
        weight_ring = weight_ring + lax.ppermute(weight_chip[d], BOTH, first_ring(d)).astype(F32)
    chip = (keep.astype(F32) + got.astype(F32)).astype(BF16).reshape(4, 16, SHARE, CHANS)
    others = [lax.ppermute(chip[d], BOTH, first_ring(d)) for d in (1, 2, 3)]
    plane = lax.all_to_all(weight_ring.astype(BF16), BOTH, 0, 0, axis_index_groups=PLANES)
    piece = plane.astype(F32).sum(0).astype(BF16)
    pieces = lax.all_to_all(
        jnp.broadcast_to(piece[None], (16, 24, CHANS)), BOTH, 0, 0, axis_index_groups=PLANES
    )
    back = feature_grads(grad4, grad_above, grad_below, conv_weight)
    others, pieces, back = lax.optimization_barrier((others, pieces, back))
    around = [lax.ppermute(pieces, BOTH, first_ring(d)) for d in (1, 2, 3)]
    ring = chip[0].astype(F32)
    for other in others:
        ring = ring + other.astype(F32)
    plane = lax.all_to_all(ring.astype(BF16), BOTH, 0, 0, axis_index_groups=PLANES)
    code_part = plane.astype(F32).sum(0)
    core = info[3]
    at = jnp.where(core == 0, info[0], info[1])
    turned = jnp.concatenate([jnp.stack(around[::-1] + [pieces])] * 2)
    mine = lax.dynamic_slice_in_dim(turned, 3 - at, 4, axis=0)
    theirs = lax.ppermute(mine, BOTH, SWAP)
    weight_grad = jnp.where(core == 0, jnp.stack([mine, theirs]), jnp.stack([theirs, mine]))
    weight_grad = weight_grad.reshape(128, 24, CHANS)[:96].reshape(96, 3, 8, CHANS)
    weight_grad = weight_grad.transpose(0, 2, 1, 3).reshape(3, CHANS, 3, CHANS)
    weight_grad = weight_grad.transpose(0, 2, 1, 3).reshape(9, CHANS, CHANS).astype(F32)
    return back.reshape(features.shape), weight_grad, code_part


def solution(mesh):
    in_specs = (
        P("clip", "tile", None, None),
        P(),
        P(),
        P(None, "clip", "tile", None),
        P("clip", "tile", None, None),
    )
    out_specs = (P("clip", "tile", None, None), P(), P(BOTH, None))
    return jax.shard_map(
        on_device, mesh=mesh, in_specs=in_specs, out_specs=out_specs, check_vma=False
    )
```

```python
import functools

import jax
import jax.numpy as jnp
from jax import lax
from jax.experimental import pallas as pl
from jax.experimental.pallas import tpu as pltpu
from jax.sharding import PartitionSpec as P

BETA = 0.25
BOTH = ("clip", "tile")
F32, BF16 = jnp.float32, jnp.bfloat16

CHANS = 256
CODES = 16384
DEPTHS = 4
COLS = 128
ROWS = 16
HERE = 2
SPOTS = HERE * ROWS * COLS
BLOCK = 4 * COLS
BLOCKS = SPOTS // BLOCK
GROUP = 16
GROUPS = DEPTHS * SPOTS // GROUP
SPILL = 64
CHUNKS = 8
UNROLL = 8
PIECES = 96
PIECE = (16, 384)
SHARE = CODES // 128


def lin(x, y, z, core):
    return (((z % 2) * 4 + y) * 2 + core) * 8 + x * 2 + z // 2


def moves(where):
    return [
        (lin(x, y, z, c), lin(*where(x, y, z, c)))
        for x in range(4)
        for y in range(4)
        for z in range(4)
        for c in range(2)
    ]


SWAP = moves(lambda x, y, z, c: (x, y, z, 1 - c))


def first_ring(d):
    return moves(lambda x, y, z, c: ((x + d) % 4, y, z, c) if c == 0 else (x, (y + d) % 4, z, c))


PLANES = [[lin(x, y, z, 0) for y in range(4) for z in range(4)] for x in range(4)] + [
    [lin(x, y, z, 1) for x in range(4) for z in range(4)] for y in range(4)
]


def place():
    clip, tile = lax.axis_index("clip"), lax.axis_index("tile")
    core, y, z_lo = clip % 2, (clip // 2) % 4, clip // 8
    x, z_hi = tile // 2, tile % 2
    return jnp.stack([x, y, z_hi * 2 + z_lo, core]).astype(jnp.int32)


def owner(x0, y0, core, j, m):
    other, z = m // 4, m % 4
    x = jnp.where(core == 0, (x0 + j) % 4, other)
    y = jnp.where(core == 0, other, (y0 + j) % 4)
    return lin(x, y, z, core)


def shifted(value, by):
    n = value.shape[0]
    col = lax.broadcasted_iota(jnp.int32, value.shape, 0) % COLS
    if by == 1:
        return jnp.where(col == 0, 0.0, pltpu.roll(value, 1, axis=0))
    return jnp.where(col == COLS - 1, 0.0, pltpu.roll(value, n - 1, axis=0))


def window_copies(above, mid, below, window, sems, first=0):
    found = []
    for n in range(HERE):
        for source, row, count in ((above, 0, 1), (mid, 1, ROWS), (below, ROWS + 1, 1)):
            found.append(
                pltpu.make_async_copy(
                    source.at[n], window.at[n, pl.ds(row, count)], sems.at[first + len(found)]
                )
            )
    return found


def list_kernel(codes, marked, spilled, count):
    cells = [codes[pl.ds(d * 32 + r, BLOCKS, stride=4), :] for r in range(4) for d in range(DEPTHS)]
    later = []
    for a in range(GROUP):
        hit = None
        for b in range(a + 1, GROUP):
            same = (cells[a] == cells[b]).astype(jnp.int32)
            hit = same if hit is None else jnp.maximum(hit, same)
        later.append(jnp.zeros_like(cells[a]) if hit is None else hit)
    flags = jnp.concatenate(later, axis=0)
    entries = jnp.concatenate(cells, axis=0)
    line = lax.broadcasted_iota(jnp.int32, (128, 128), 0)
    lane = lax.broadcasted_iota(jnp.int32, (128, 128), 1)
    bits = flags.astype(F32)
    inside = jnp.dot(bits, (line < lane).astype(F32), preferred_element_type=F32)
    per_row = jnp.dot(bits, jnp.ones((128, 128), F32), preferred_element_type=F32)
    ahead = jnp.dot((lane < line).astype(F32), per_row, preferred_element_type=F32)
    rank = (inside + ahead).astype(jnp.int32)
    marked[...] = 2 * jnp.where(flags > 0, CODES + rank, entries)
    rank = jnp.where(flags > 0, rank, -1)
    for s in range(SPILL):
        spilled[pl.ds(s, 1), :] = jnp.sum(
            jnp.where(rank == s, 2 * entries, 0), axis=0, keepdims=True
        )
    spilled[...] = jnp.broadcast_to(
        jnp.sum(spilled[...].astype(F32), axis=1, keepdims=True), (SPILL, 128)
    ).astype(jnp.int32)
    whole = jnp.sum(per_row, axis=0, keepdims=True).astype(jnp.int32)
    count[...] = jnp.broadcast_to(whole, (8, 128))


def entry_lists(codes):
    ints = jnp.int32
    return pl.pallas_call(
        list_kernel,
        out_shape=[
            jax.ShapeDtypeStruct((128, 128), ints),
            jax.ShapeDtypeStruct((SPILL, 128), ints),
            jax.ShapeDtypeStruct((8, 128), ints),
        ],
    )(codes.reshape(128, 128))


def quantizer_kernel(
    spilled, info, count,
    marked, plain, codebook, feats, above, below, weights, up,
    grad, send, keep, weight_send, weight_keep,
    table, sums, lat, raw, near, taps, window, weight_sum, weight_out, ids, sems,
):
    many = count[0, 0]
    windows = window_copies(above, feats, below, window, sems)
    get_taps = pltpu.make_async_copy(weights, taps, sems.at[6])
    get_ids = pltpu.make_async_copy(marked, ids, sems.at[7])
    get_up = pltpu.make_async_copy(up, near, sems.at[8])
    chunk = CODES // CHUNKS

    def get_table(c):
        rows = pl.ds(c * chunk, chunk)
        return pltpu.make_async_copy(codebook.at[rows], raw.at[rows], sems.at[16 + c])

    for copy in windows + [get_taps]:
        copy.start()
    for c in range(CHUNKS):
        get_table(c).start()
    get_ids.start()
    get_up.start()
    for copy in windows + [get_taps]:
        copy.wait()

    def convolve(block, carry):
        clip = block // (ROWS // 4)
        row = (block % (ROWS // 4)) * 4
        cols = [None] * 3
        for a in range(3):
            part = window[clip, pl.ds(row + a, 4)].reshape(BLOCK, CHANS)
            for b in range(3):
                term = jnp.dot(part, taps[3 * a + b], preferred_element_type=F32)
                cols[b] = term if a == 0 else cols[b] + term
        latent = shifted(cols[0], 1) + cols[1] + shifted(cols[2], -1)
        for r in range(4):
            at = pl.multiple_of(block * (2 * BLOCK), 8) + 2 * r
            own = latent[r * COLS : (r + 1) * COLS]
            lat[pl.ds(at, COLS, stride=8), :] = own[:, :128]
            lat[pl.ds(at + 1, COLS, stride=8), :] = own[:, 128:]
        return carry

    lax.fori_loop(0, BLOCKS, convolve, 0)

    for c in range(CHUNKS):
        get_table(c).wait()

        def convert(t, carry):
            at = pl.multiple_of(c * chunk + t * 512, 16)
            part = raw[pl.ds(at, 512), :].astype(F32)
            at = pl.multiple_of(2 * at, 8)
            table[pl.ds(at, 512, stride=2), :] = part[:, :128]
            table[pl.ds(at + 1, 512, stride=2), :] = part[:, 128:]
            sums[pl.ds(at, 1024), :] = jnp.zeros((1024, 128), F32)
            return carry

        lax.fori_loop(0, chunk // 512, convert, 0)

    sums[pl.ds(2 * CODES, 2 * SPILL), :] = jnp.zeros((2 * SPILL, 128), F32)

    def lend(s, carry):
        table[pl.ds(2 * (CODES + s), 2), :] = table[pl.ds(spilled[s, 0], 2), :]
        return carry

    lax.fori_loop(0, jnp.minimum(many, SPILL), lend, 0)

    def resids(group, code):
        found = []
        first = pl.multiple_of(group * 8, 8)
        for r in range(4):
            here = pl.ds(first + 2 * r, 2)
            resid, total = lat[here, :], None
            for d in range(DEPTHS):
                k = code(r, d)
                resid = resid - table[pl.ds(k, 2), :]
                total = resid if total is None else total + resid
                found.append((k, resid))
            lat[here, :] = total
        return found

    get_ids.wait()

    @pl.when(many <= SPILL)
    def _():
        def blocks(block, carry):
            def step(col, carry):
                first = block * COLS + col
                found = resids(first, lambda r, d: ids[first + (r * DEPTHS + d) * GROUPS])
                new = [sums[pl.ds(k, 2), :] + v for k, v in found]
                for (k, _), v in zip(found, new):
                    sums[pl.ds(k, 2), :] = v
                return carry

            return lax.fori_loop(0, COLS, step, carry, unroll=UNROLL)

        lax.fori_loop(0, BLOCKS, blocks, 0)

        def give_back(s, carry):
            k = spilled[s, 0]
            sums[pl.ds(k, 2), :] = sums[pl.ds(k, 2), :] + sums[pl.ds(2 * (CODES + s), 2), :]
            return carry

        lax.fori_loop(0, many, give_back, 0)

    @pl.when(many > SPILL)
    def _():
        again = pltpu.make_async_copy(plain, ids, sems.at[7])
        again.start()
        again.wait()

        def blocks(block, carry):
            def step(col, carry):
                spot = block * BLOCK + col
                for k, v in resids(block * COLS + col, lambda r, d: 2 * ids[d * SPOTS + spot + r * COLS]):
                    sums[pl.ds(k, 2), :] = sums[pl.ds(k, 2), :] + v
                return carry

            return lax.fori_loop(0, COLS, step, carry)

        lax.fori_loop(0, BLOCKS, blocks, 0)

    get_up.wait()

    def put_grad(block):
        rows = pl.ds(pl.multiple_of(block * BLOCK, 16), BLOCK)
        return pltpu.make_async_copy(near.at[rows], grad.at[rows], sems.at[8 + block])

    def gradient(block, carry):
        rows = pl.ds(pl.multiple_of(block * BLOCK, 16), BLOCK)
        at = pl.multiple_of(block * (2 * BLOCK), 8)
        halves = [
            jnp.concatenate([lat[pl.ds(at + 2 * r + h, COLS, stride=8), :] for r in range(4)], axis=0)
            for h in range(2)
        ]
        total = jnp.concatenate(halves, axis=1)
        near[rows, :] = (near[rows, :].astype(F32) + 2.0 * BETA * total).astype(BF16)
        put_grad(block).start()
        return carry

    lax.fori_loop(0, BLOCKS, gradient, 0)

    def put_out(out, first, j):
        rows = pl.ds((first + j) * 16 * SHARE, 16 * SHARE)
        return pltpu.make_async_copy(raw.at[rows], out.at[j], sems.at[16 + first + j])

    def fill(m, carry, first, core, j):
        at = pl.multiple_of(owner(info[0], info[1], core, j, m) * (2 * SHARE), 8)
        rows = pl.ds(pl.multiple_of(((first + j) * 16 + m) * SHARE, 16), SHARE)
        raw[rows, :128] = (sums[pl.ds(at, SHARE, stride=2), :] * -2.0).astype(BF16)
        raw[rows, 128:] = (sums[pl.ds(at + 1, SHARE, stride=2), :] * -2.0).astype(BF16)
        return carry

    for first, core, out in ((0, 1 - info[3], send), (4, info[3], keep)):
        for j in range(4):
            lax.fori_loop(0, 16, functools.partial(fill, first=first, core=core, j=j), 0, unroll=2)
            put_out(out, first, j).start()

    weight_sum[...] = jnp.zeros_like(weight_sum)

    def weigh(block, carry):
        clip = block // (ROWS // 4)
        row = (block % (ROWS // 4)) * 4
        own = near[pl.ds(pl.multiple_of(block * BLOCK, 16), BLOCK), :]
        mid = own.astype(F32)
        wide = jnp.concatenate(
            [shifted(mid, -1).astype(BF16), own, shifted(mid, 1).astype(BF16)], axis=1
        )
        for a in range(3):
            part = window[clip, pl.ds(row + a, 4)].reshape(BLOCK, CHANS)
            weight_sum[pl.ds(a * CHANS, CHANS), :] += lax.dot_general(
                part, wide, (((0,), (0,)), ((), ())), preferred_element_type=F32
            )
        return carry

    lax.fori_loop(0, BLOCKS, weigh, 0)

    def cut(m, carry, side, core, j):
        near_by = jnp.where(core == 0, info[0], info[1])
        b = jnp.minimum(core * 64 + (near_by + j) % 4 * 16 + m, PIECES - 1)
        rows = weight_sum[pl.ds(pl.multiple_of(b * 8, 8), 8), :]
        both = jnp.concatenate([rows[:, :384], rows[:, 384:]], axis=0)
        weight_out[side, j, m] = both.astype(BF16)
        return carry

    def put_weights(out, side):
        return pltpu.make_async_copy(weight_out.at[side], out, sems.at[24 + side])

    for side, core, out in ((0, 1 - info[3], weight_send), (1, info[3], weight_keep)):
        for j in range(4):
            lax.fori_loop(0, 16, functools.partial(cut, side=side, core=core, j=j), 0, unroll=4)
        put_weights(out, side).start()
    for block in range(BLOCKS):
        put_grad(block).wait()
    for first, out in ((0, send), (4, keep)):
        for j in range(4):
            put_out(out, first, j).wait()
    put_weights(weight_send, 0).wait()
    put_weights(weight_keep, 1).wait()


def quantizer(marked, plain, spilled, info, count, codebook, feats, above, below, weights, up):
    hbm = pl.BlockSpec(memory_space=pl.ANY)
    smem = pl.BlockSpec(memory_space=pltpu.SMEM)
    out_shape = (4, 16 * SHARE, CHANS)
    weight_shape = (4, 16) + PIECE
    return pl.pallas_call(
        quantizer_kernel,
        in_specs=[smem] * 3 + [hbm] * 8,
        out_specs=[hbm] * 5,
        scratch_shapes=[
            pltpu.VMEM((2 * (CODES + SPILL), 128), F32),
            pltpu.VMEM((2 * (CODES + SPILL), 128), F32),
            pltpu.VMEM((2 * SPOTS, 128), F32),
            pltpu.VMEM((CODES, CHANS), BF16),
            pltpu.VMEM((SPOTS, CHANS), BF16),
            pltpu.VMEM((9, CHANS, CHANS), BF16),
            pltpu.VMEM((HERE, ROWS + 2, COLS, CHANS), BF16),
            pltpu.VMEM((3 * CHANS, 3 * CHANS), F32),
            pltpu.VMEM((2,) + weight_shape, BF16),
            pltpu.SMEM((DEPTHS * SPOTS,), jnp.int32),
            pltpu.SemaphoreType.DMA((26,)),
        ],
        out_shape=[
            jax.ShapeDtypeStruct((SPOTS, CHANS), BF16),
            jax.ShapeDtypeStruct(out_shape, BF16),
            jax.ShapeDtypeStruct(out_shape, BF16),
            jax.ShapeDtypeStruct(weight_shape, BF16),
            jax.ShapeDtypeStruct(weight_shape, BF16),
        ],
        compiler_params=pltpu.CompilerParams(vmem_limit_bytes=58 << 20),
        cost_estimate=pl.CostEstimate(
            flops=4 * 9 * SPOTS * CHANS * CHANS, bytes_accessed=64 << 20, transcendentals=0
        ),
    )(spilled, info, count, marked, plain, codebook, feats, above, below, weights, up)


def back_kernel(grad, above, below, weights, out, window, sems):
    i = pl.program_id(0)

    copies = window_copies(above, grad, below, window, sems)

    @pl.when(i == 0)
    def _():
        for copy in copies:
            copy.start()
        for copy in copies:
            copy.wait()

    clip = i // (ROWS // 4)
    row = (i % (ROWS // 4)) * 4
    cols = [None] * 3
    for a in range(3):
        part = window[clip, pl.ds(row + 2 - a, 4)].reshape(BLOCK, CHANS)
        for b in range(3):
            term = lax.dot_general(
                part, weights[3 * a + b], (((1,), (1,)), ((), ())), preferred_element_type=F32
            )
            cols[b] = term if a == 0 else cols[b] + term
    back = shifted(cols[0], -1) + cols[1] + shifted(cols[2], 1)
    out[...] = back.astype(BF16)


def feature_grads(grad, above, below, weights):
    return pl.pallas_call(
        back_kernel,
        grid=(BLOCKS,),
        in_specs=[
            pl.BlockSpec(memory_space=pl.ANY),
            pl.BlockSpec(memory_space=pl.ANY),
            pl.BlockSpec(memory_space=pl.ANY),
            pl.BlockSpec((9, CHANS, CHANS), lambda i: (0, 0, 0)),
        ],
        out_specs=pl.BlockSpec((BLOCK, CHANS), lambda i: (i, 0)),
        scratch_shapes=[
            pltpu.VMEM((HERE, ROWS + 2, COLS, CHANS), BF16),
            pltpu.SemaphoreType.DMA((3 * HERE,)),
        ],
        out_shape=jax.ShapeDtypeStruct((SPOTS, CHANS), BF16),
        compiler_params=pltpu.CompilerParams(
            vmem_limit_bytes=32 << 20, dimension_semantics=("arbitrary",)
        ),
        cost_estimate=pl.CostEstimate(
            flops=2 * 9 * SPOTS * CHANS * CHANS, bytes_accessed=8 << 20, transcendentals=0
        ),
    )(grad, above, below, weights)


def turn_kernel(info, *refs):
    at = jnp.where(info[3] == 0, info[0], info[1])
    for d in range(4):
        refs[4][(at + 4 - d) % 4] = refs[d][...]


def turned(info, pieces, around):
    return pl.pallas_call(
        turn_kernel,
        in_specs=[pl.BlockSpec(memory_space=pltpu.SMEM)] + [pl.BlockSpec()] * 4,
        out_shape=jax.ShapeDtypeStruct((4,) + pieces.shape, BF16),
    )(info, pieces, *around)


def join_kernel(info, mine, theirs, out):
    def join(low, high):
        for a in range(3):
            for r in range(2):

                def place(m, carry):
                    ref, ring = (low, 2 * a + r) if a < 2 else (high, r)
                    both = ref[ring, m].astype(F32)
                    top, bottom = both[:8], both[8:]
                    rows = pl.ds(pl.multiple_of((r * 16 + m) * 8, 8), 8)
                    out[3 * a, rows, :] = top[:, :256]
                    out[3 * a + 1, rows, :128] = top[:, 256:]
                    out[3 * a + 1, rows, 128:] = bottom[:, :128]
                    out[3 * a + 2, rows, :] = bottom[:, 128:]
                    return carry

                lax.fori_loop(0, 16, place, 0, unroll=4)

    @pl.when(info[3] == 0)
    def _():
        join(mine, theirs)

    @pl.when(info[3] != 0)
    def _():
        join(theirs, mine)


def joined(info, mine, theirs):
    return pl.pallas_call(
        join_kernel,
        in_specs=[pl.BlockSpec(memory_space=pltpu.SMEM)] + [pl.BlockSpec()] * 2,
        out_shape=jax.ShapeDtypeStruct((9, CHANS, CHANS), F32),
        compiler_params=pltpu.CompilerParams(vmem_limit_bytes=32 << 20),
    )(info, mine, theirs)


def edges(array):
    n = lax.axis_size("tile")
    up = [(i, i + 1) for i in range(n - 1)]
    down = [(i + 1, i) for i in range(n - 1)]
    above = lax.ppermute(array[:, -1:], "tile", up)
    below = lax.ppermute(array[:, :1], "tile", down)
    return above, below


def on_device(features, conv_weight, codebook, codes, upstream):
    info = place()
    above, below = edges(features)
    marked, spilled, count = entry_lists(codes)
    grad, send, keep, weight_send, weight_keep = quantizer(
        marked.reshape(-1), codes.reshape(-1), spilled, info, count, codebook, features, above,
        below, conv_weight, upstream.reshape(SPOTS, CHANS),
    )
    got = lax.ppermute(send, BOTH, SWAP)
    grad4 = grad.reshape(features.shape)
    grad_above, grad_below = edges(grad4)
    weight_got = lax.ppermute(weight_send, BOTH, SWAP)
    weight_chip = (weight_keep.astype(F32) + weight_got.astype(F32)).astype(BF16)
    keep, got, grad_above, grad_below = lax.optimization_barrier(
        (keep, got, grad_above, grad_below)
    )
    weight_ring = weight_chip[0].astype(F32)
    for d in (1, 2, 3):
        weight_ring = weight_ring + lax.ppermute(weight_chip[d], BOTH, first_ring(d)).astype(F32)
    chip = (keep.astype(F32) + got.astype(F32)).astype(BF16).reshape(4, 16, SHARE, CHANS)
    others = [lax.ppermute(chip[d], BOTH, first_ring(d)) for d in (1, 2, 3)]
    plane = lax.all_to_all(weight_ring.astype(BF16), BOTH, 0, 0, axis_index_groups=PLANES)
    piece = plane.astype(F32).sum(0).astype(BF16)
    piece, grad_above = lax.optimization_barrier((piece, grad_above))
    pieces = lax.all_to_all(
        jnp.broadcast_to(piece[None], (16,) + PIECE), BOTH, 0, 0, axis_index_groups=PLANES
    )
    back = feature_grads(grad4, grad_above, grad_below, conv_weight)
    ring = chip[0].astype(F32)
    for other in others:
        ring = ring + other.astype(F32)
    ring, pieces, back = lax.optimization_barrier((ring.astype(BF16), pieces, back))
    plane = lax.all_to_all(ring, BOTH, 0, 0, axis_index_groups=PLANES)
    around = [lax.ppermute(pieces, BOTH, first_ring(d)) for d in (1, 2, 3)]
    mine = turned(info, pieces, around)
    theirs = lax.ppermute(mine, BOTH, SWAP)
    code_part = plane.astype(F32).sum(0)
    return back.reshape(features.shape), joined(info, mine, theirs), code_part


def solution(mesh):
    in_specs = (
        P("clip", "tile", None, None),
        P(),
        P(),
        P(None, "clip", "tile", None),
        P("clip", "tile", None, None),
    )
    out_specs = (P("clip", "tile", None, None), P(), P(BOTH, None))
    return jax.shard_map(
        on_device, mesh=mesh, in_specs=in_specs, out_specs=out_specs, check_vma=False
    )
```

```python
import functools

import jax
import jax.numpy as jnp
from jax import lax
from jax.experimental import pallas as pl
from jax.experimental.pallas import tpu as pltpu
from jax.sharding import PartitionSpec as P

BETA = 0.25
BOTH = ("clip", "tile")
F32, BF16 = jnp.float32, jnp.bfloat16

CHANS = 256
CODES = 16384
DEPTHS = 4
COLS = 128
ROWS = 16
HERE = 2
SPOTS = HERE * ROWS * COLS
BLOCK = 4 * COLS
BLOCKS = SPOTS // BLOCK
TALL = 4
GROUP = TALL * DEPTHS
STRIPS = SPOTS // (TALL * COLS)
GROUPS = DEPTHS * SPOTS // GROUP
SPILL = 64
CHUNKS = 8
UNROLL = 8
PIECES = 96
PIECE = (16, 384)
SHARE = CODES // 128


def lin(x, y, z, core):
    return (((z % 2) * 4 + y) * 2 + core) * 8 + x * 2 + z // 2


def moves(where):
    return [
        (lin(x, y, z, c), lin(*where(x, y, z, c)))
        for x in range(4)
        for y in range(4)
        for z in range(4)
        for c in range(2)
    ]


SWAP = moves(lambda x, y, z, c: (x, y, z, 1 - c))


def first_ring(d):
    return moves(lambda x, y, z, c: ((x + d) % 4, y, z, c) if c == 0 else (x, (y + d) % 4, z, c))


PLANES = [[lin(x, y, z, 0) for y in range(4) for z in range(4)] for x in range(4)] + [
    [lin(x, y, z, 1) for x in range(4) for z in range(4)] for y in range(4)
]


def place():
    clip, tile = lax.axis_index("clip"), lax.axis_index("tile")
    core, y, z_lo = clip % 2, (clip // 2) % 4, clip // 8
    x, z_hi = tile // 2, tile % 2
    return jnp.stack([x, y, z_hi * 2 + z_lo, core, tile, lax.axis_size("tile")]).astype(jnp.int32)


def owner(x0, y0, core, j, m):
    other, z = m // 4, m % 4
    x = jnp.where(core == 0, (x0 + j) % 4, other)
    y = jnp.where(core == 0, other, (y0 + j) % 4)
    return lin(x, y, z, core)


def shifted(value, by):
    n = value.shape[0]
    col = lax.broadcasted_iota(jnp.int32, value.shape, 0) % COLS
    if by == 1:
        return jnp.where(col == 0, 0.0, pltpu.roll(value, 1, axis=0))
    return jnp.where(col == COLS - 1, 0.0, pltpu.roll(value, n - 1, axis=0))


def window_copies(above, mid, below, window, sems, first=0):
    found = []
    for n in range(HERE):
        for source, row, count in ((above, 0, 1), (mid, 1, ROWS), (below, ROWS + 1, 1)):
            found.append(
                pltpu.make_async_copy(
                    source.at[n], window.at[n, pl.ds(row, count)], sems.at[first + len(found)]
                )
            )
    return found


def list_kernel(codes, marked, extra, parts):
    cells = [
        codes[pl.ds(d * HERE * ROWS + r, STRIPS, stride=TALL), :]
        for r in range(TALL)
        for d in range(DEPTHS)
    ]
    later = []
    for a in range(GROUP):
        hit = None
        for b in range(a + 1, GROUP):
            same = (cells[a] == cells[b]).astype(jnp.int32)
            hit = same if hit is None else jnp.maximum(hit, same)
        later.append(jnp.zeros_like(cells[a]) if hit is None else hit)
    flags = jnp.concatenate(later, axis=0)
    entries = jnp.concatenate(cells, axis=0)
    line = lax.broadcasted_iota(jnp.int32, (128, 128), 0)
    lane = lax.broadcasted_iota(jnp.int32, (128, 128), 1)
    bits = flags.astype(F32)
    inside = jnp.dot(bits, (line < lane).astype(F32), preferred_element_type=F32)
    per_row = jnp.dot(bits, jnp.ones((128, 128), F32), preferred_element_type=F32)
    ahead = jnp.dot((lane < line).astype(F32), per_row, preferred_element_type=F32)
    rank = (inside + ahead).astype(jnp.int32)
    marked[...] = 2 * jnp.where(flags > 0, CODES + rank, entries)
    rank = jnp.where(flags > 0, rank, -1)
    for s in range(SPILL):
        parts[pl.ds(s, 1), :] = jnp.sum(
            jnp.where(rank == s, 2 * entries, 0), axis=0, keepdims=True
        )
    codes_of = jnp.sum(parts[...].astype(F32), axis=1, keepdims=True)
    square = lax.broadcasted_iota(jnp.int32, (SPILL, 128), 0) == lax.broadcasted_iota(
        jnp.int32, (SPILL, 128), 1
    )
    spilled = jnp.sum(jnp.where(square, codes_of, 0.0), axis=0, keepdims=True)
    whole = jnp.sum(per_row, axis=0, keepdims=True)
    both = jnp.concatenate([jnp.broadcast_to(spilled, (4, 128)), jnp.broadcast_to(whole, (4, 128))])
    extra[...] = both.astype(jnp.int32)


def entry_lists(codes):
    ints = jnp.int32
    return pl.pallas_call(
        list_kernel,
        out_shape=[
            jax.ShapeDtypeStruct((128, 128), ints),
            jax.ShapeDtypeStruct((8, 128), ints),
        ],
        scratch_shapes=[pltpu.VMEM((SPILL, 128), ints)],
    )(codes.reshape(128, 128))


def quantizer_kernel(
    extra, info,
    marked, plain, codebook, feats, above, below, weights, up,
    grad, grad_first, grad_last, send, keep, weight_send, weight_keep,
    table, sums, lat, raw, near, taps, window, weight_sum, weight_out, all_ids, sems, *ids,
):
    many = extra[4, 0]
    windows = window_copies(above, feats, below, window, sems)
    get_taps = pltpu.make_async_copy(weights, taps, sems.at[6])
    get_ids = [
        pltpu.make_async_copy(marked.at[pl.ds(c * GROUPS, GROUPS)], ids[c], sems.at[26 + c])
        for c in range(GROUP)
    ]
    get_up = pltpu.make_async_copy(up, near, sems.at[8])
    chunk = CODES // CHUNKS

    def get_table(c):
        rows = pl.ds(c * chunk, chunk)
        return pltpu.make_async_copy(codebook.at[rows], raw.at[rows], sems.at[16 + c])

    early = [get_taps] + windows[:3]
    for copy in early + windows[3:]:
        copy.start()
    for copy in early + windows[3:]:
        copy.wait()
    close_frame(info, window)
    for c in range(CHUNKS):
        get_table(c).start()
    for copy in get_ids + [get_up]:
        copy.start()

    def line(block, r):
        row = block * 4 + r
        return pl.multiple_of(row // TALL * (2 * TALL * COLS), 8) + 2 * (row % TALL)

    def convolve(block, carry):
        clip = block // (ROWS // 4)
        row = (block % (ROWS // 4)) * 4
        cols = [None] * 3
        for a in range(3):
            part = window[clip, pl.ds(row + a, 4)].reshape(BLOCK, CHANS)
            for b in range(3):
                term = jnp.dot(part, taps[3 * a + b], preferred_element_type=F32)
                cols[b] = term if a == 0 else cols[b] + term
        latent = shifted(cols[0], 1) + cols[1] + shifted(cols[2], -1)
        for r in range(4):
            at = line(block, r)
            own = latent[r * COLS : (r + 1) * COLS]
            lat[pl.ds(at, COLS, stride=2 * TALL), :] = own[:, :128]
            lat[pl.ds(at + 1, COLS, stride=2 * TALL), :] = own[:, 128:]
        return carry

    lax.fori_loop(0, BLOCKS, convolve, 0)

    for c in range(CHUNKS):
        get_table(c).wait()

        def convert(t, carry):
            at = pl.multiple_of(c * chunk + t * 512, 16)
            part = raw[pl.ds(at, 512), :].astype(F32)
            at = pl.multiple_of(2 * at, 8)
            table[pl.ds(at, 512, stride=2), :] = part[:, :128]
            table[pl.ds(at + 1, 512, stride=2), :] = part[:, 128:]
            sums[pl.ds(at, 1024), :] = jnp.zeros((1024, 128), F32)
            return carry

        lax.fori_loop(0, chunk // 512, convert, 0)

    sums[pl.ds(2 * CODES, 2 * SPILL), :] = jnp.zeros((2 * SPILL, 128), F32)

    def lend(s, carry):
        table[pl.ds(2 * (CODES + s), 2), :] = table[pl.ds(extra[0, s], 2), :]
        return carry

    lax.fori_loop(0, jnp.minimum(many, SPILL), lend, 0)

    def resids(group, code):
        found = []
        first = pl.multiple_of(group * (2 * TALL), 8)
        for r in range(TALL):
            here = pl.ds(first + 2 * r, 2)
            resid, total = lat[here, :], None
            for d in range(DEPTHS):
                k = code(r, d)
                resid = resid - table[pl.ds(k, 2), :]
                total = resid if total is None else total + resid
                found.append((k, resid))
            lat[here, :] = total
        return found

    for copy in get_ids:
        copy.wait()

    @pl.when(many <= SPILL)
    def _():
        def blocks(block, carry):
            def step(col, carry):
                first = block * COLS + col
                found = resids(first, lambda r, d: ids[r * DEPTHS + d][first])
                new = [sums[pl.ds(k, 2), :] + v for k, v in found]
                for (k, _), v in zip(found, new):
                    sums[pl.ds(k, 2), :] = v
                return carry

            return lax.fori_loop(0, COLS, step, carry, unroll=UNROLL)

        lax.fori_loop(0, STRIPS, blocks, 0)

        def give_back(s, carry):
            k = extra[0, s]
            sums[pl.ds(k, 2), :] = sums[pl.ds(k, 2), :] + sums[pl.ds(2 * (CODES + s), 2), :]
            return carry

        lax.fori_loop(0, many, give_back, 0)

    @pl.when(many > SPILL)
    def _():
        again = pltpu.make_async_copy(plain, all_ids, sems.at[7])
        again.start()
        again.wait()

        def blocks(block, carry):
            def step(col, carry):
                spot = block * (TALL * COLS) + col
                for k, v in resids(block * COLS + col, lambda r, d: 2 * all_ids[d * SPOTS + spot + r * COLS]):
                    sums[pl.ds(k, 2), :] = sums[pl.ds(k, 2), :] + v
                return carry

            return lax.fori_loop(0, COLS, step, carry)

        lax.fori_loop(0, STRIPS, blocks, 0)

    get_up.wait()

    def put_grad(block):
        rows = pl.ds(pl.multiple_of(block * BLOCK, 16), BLOCK)
        return pltpu.make_async_copy(near.at[rows], grad.at[rows], sems.at[8 + block])

    def gradient(block, carry):
        rows = pl.ds(pl.multiple_of(block * BLOCK, 16), BLOCK)
        halves = [
            jnp.concatenate(
                [lat[pl.ds(line(block, r) + h, COLS, stride=2 * TALL), :] for r in range(4)], axis=0
            )
            for h in range(2)
        ]
        total = jnp.concatenate(halves, axis=1)
        near[rows, :] = (near[rows, :].astype(F32) + 2.0 * BETA * total).astype(BF16)
        put_grad(block).start()
        return carry

    lax.fori_loop(0, BLOCKS, gradient, 0)
    put_edges = []
    for out, row in ((grad_first, 0), (grad_last, ROWS - 1)):
        for n in range(HERE):
            rows = pl.ds((n * ROWS + row) * COLS, COLS)
            put_edges.append(
                pltpu.make_async_copy(
                    near.at[rows], out.at[n, 0], sems.at[26 + GROUP + len(put_edges)]
                )
            )
    for copy in put_edges:
        copy.start()

    def put_out(out, first, j):
        rows = pl.ds((first + j) * 16 * SHARE, 16 * SHARE)
        return pltpu.make_async_copy(raw.at[rows], out.at[j], sems.at[16 + first + j])

    def fill(m, carry, first, core, j):
        at = pl.multiple_of(owner(info[0], info[1], core, j, m) * (2 * SHARE), 8)
        rows = pl.ds(pl.multiple_of(((first + j) * 16 + m) * SHARE, 16), SHARE)
        raw[rows, :128] = (sums[pl.ds(at, SHARE, stride=2), :] * -2.0).astype(BF16)
        raw[rows, 128:] = (sums[pl.ds(at + 1, SHARE, stride=2), :] * -2.0).astype(BF16)
        return carry

    for first, core, out in ((0, 1 - info[3], send), (4, info[3], keep)):
        for j in range(4):
            lax.fori_loop(0, 16, functools.partial(fill, first=first, core=core, j=j), 0, unroll=2)
            put_out(out, first, j).start()

    weight_sum[...] = jnp.zeros_like(weight_sum)

    def weigh(block, carry):
        clip = block // (ROWS // 4)
        row = (block % (ROWS // 4)) * 4
        own = near[pl.ds(pl.multiple_of(block * BLOCK, 16), BLOCK), :]
        mid = own.astype(F32)
        wide = jnp.concatenate(
            [shifted(mid, -1).astype(BF16), own, shifted(mid, 1).astype(BF16)], axis=1
        )
        for a in range(3):
            part = window[clip, pl.ds(row + a, 4)].reshape(BLOCK, CHANS)
            weight_sum[pl.ds(a * CHANS, CHANS), :] += lax.dot_general(
                part, wide, (((0,), (0,)), ((), ())), preferred_element_type=F32
            )
        return carry

    lax.fori_loop(0, BLOCKS, weigh, 0)

    def cut(side, core, j):
        ring = (jnp.where(core == 0, info[0], info[1]) + j) % 4
        first = pl.multiple_of(jnp.minimum(core * 64 + ring * 16, PIECES - 16) * 8, 128)
        for m in range(16):
            rows = weight_sum[pl.ds(first + 8 * m, 8), :]
            both = jnp.concatenate([rows[:, :384], rows[:, 384:]], axis=0)
            weight_out[side, j, m] = both.astype(BF16)

    def put_weights(out, side):
        return pltpu.make_async_copy(weight_out.at[side], out, sems.at[24 + side])

    for side, core, out in ((0, 1 - info[3], weight_send), (1, info[3], weight_keep)):
        for j in range(4):
            cut(side, core, j)
        put_weights(out, side).start()
    for copy in put_edges:
        copy.wait()
    for block in range(BLOCKS):
        put_grad(block).wait()
    for first, out in ((0, send), (4, keep)):
        for j in range(4):
            put_out(out, first, j).wait()
    put_weights(weight_send, 0).wait()
    put_weights(weight_keep, 1).wait()


def quantizer(marked, plain, extra, info, codebook, feats, above, below, weights, up):
    hbm = pl.BlockSpec(memory_space=pl.ANY)
    smem = pl.BlockSpec(memory_space=pltpu.SMEM)
    out_shape = (4, 16 * SHARE, CHANS)
    weight_shape = (4, 16) + PIECE
    return pl.pallas_call(
        quantizer_kernel,
        in_specs=[smem] * 2 + [hbm] * 8,
        out_specs=[hbm] * 7,
        scratch_shapes=[
            pltpu.VMEM((2 * (CODES + SPILL), 128), F32),
            pltpu.VMEM((2 * (CODES + SPILL), 128), F32),
            pltpu.VMEM((2 * SPOTS, 128), F32),
            pltpu.VMEM((CODES, CHANS), BF16),
            pltpu.VMEM((SPOTS, CHANS), BF16),
            pltpu.VMEM((9, CHANS, CHANS), BF16),
            pltpu.VMEM((HERE, ROWS + 2, COLS, CHANS), BF16),
            pltpu.VMEM((3 * CHANS, 3 * CHANS), F32),
            pltpu.VMEM((2,) + weight_shape, BF16),
            pltpu.SMEM((DEPTHS * SPOTS,), jnp.int32),
            pltpu.SemaphoreType.DMA((26 + GROUP + 2 * HERE,)),
        ]
        + [pltpu.SMEM((GROUPS,), jnp.int32)] * GROUP,
        out_shape=[
            jax.ShapeDtypeStruct((SPOTS, CHANS), BF16),
            jax.ShapeDtypeStruct((HERE, 1, COLS, CHANS), BF16),
            jax.ShapeDtypeStruct((HERE, 1, COLS, CHANS), BF16),
            jax.ShapeDtypeStruct(out_shape, BF16),
            jax.ShapeDtypeStruct(out_shape, BF16),
            jax.ShapeDtypeStruct(weight_shape, BF16),
            jax.ShapeDtypeStruct(weight_shape, BF16),
        ],
        compiler_params=pltpu.CompilerParams(vmem_limit_bytes=58 << 20),
        cost_estimate=pl.CostEstimate(
            flops=4 * 9 * SPOTS * CHANS * CHANS, bytes_accessed=64 << 20, transcendentals=0
        ),
    )(extra, info, marked, plain, codebook, feats, above, below, weights, up)


def back_kernel(info, grad, above, below, weights, out, window, sems):
    i = pl.program_id(0)

    copies = window_copies(above, grad, below, window, sems)

    @pl.when(i == 0)
    def _():
        for copy in copies:
            copy.start()
        for copy in copies:
            copy.wait()
        close_frame(info, window)

    clip = i // (ROWS // 4)
    row = (i % (ROWS // 4)) * 4
    cols = [None] * 3
    for a in range(3):
        part = window[clip, pl.ds(row + 2 - a, 4)].reshape(BLOCK, CHANS)
        for b in range(3):
            term = lax.dot_general(
                part, weights[3 * a + b], (((1,), (1,)), ((), ())), preferred_element_type=F32
            )
            cols[b] = term if a == 0 else cols[b] + term
    back = shifted(cols[0], -1) + cols[1] + shifted(cols[2], 1)
    out[...] = back.astype(BF16)


def feature_grads(info, grad, above, below, weights):
    return pl.pallas_call(
        back_kernel,
        grid=(BLOCKS,),
        in_specs=[
            pl.BlockSpec(memory_space=pltpu.SMEM),
            pl.BlockSpec(memory_space=pl.ANY),
            pl.BlockSpec(memory_space=pl.ANY),
            pl.BlockSpec(memory_space=pl.ANY),
            pl.BlockSpec((9, CHANS, CHANS), lambda i: (0, 0, 0)),
        ],
        out_specs=pl.BlockSpec((BLOCK, CHANS), lambda i: (i, 0)),
        scratch_shapes=[
            pltpu.VMEM((HERE, ROWS + 2, COLS, CHANS), BF16),
            pltpu.SemaphoreType.DMA((3 * HERE,)),
        ],
        out_shape=jax.ShapeDtypeStruct((SPOTS, CHANS), BF16),
        compiler_params=pltpu.CompilerParams(
            vmem_limit_bytes=32 << 20, dimension_semantics=("arbitrary",)
        ),
        cost_estimate=pl.CostEstimate(
            flops=2 * 9 * SPOTS * CHANS * CHANS, bytes_accessed=8 << 20, transcendentals=0
        ),
    )(info, grad, above, below, weights)


def turn_kernel(info, *refs):
    at = jnp.where(info[3] == 0, info[0], info[1])
    for d in range(4):
        refs[4][(at + 4 - d) % 4] = refs[d][...]


def turned(info, pieces, around):
    return pl.pallas_call(
        turn_kernel,
        in_specs=[pl.BlockSpec(memory_space=pltpu.SMEM)] + [pl.BlockSpec()] * 4,
        out_shape=jax.ShapeDtypeStruct((4,) + pieces.shape, BF16),
    )(info, pieces, *around)


def join_kernel(info, mine, theirs, out):
    def join(low, high):
        for a in range(3):
            for r in range(2):

                def place(m, carry):
                    ref, ring = (low, 2 * a + r) if a < 2 else (high, r)
                    both = ref[ring, m].astype(F32)
                    top, bottom = both[:8], both[8:]
                    rows = pl.ds(pl.multiple_of((r * 16 + m) * 8, 8), 8)
                    out[3 * a, rows, :] = top[:, :256]
                    out[3 * a + 1, rows, :128] = top[:, 256:]
                    out[3 * a + 1, rows, 128:] = bottom[:, :128]
                    out[3 * a + 2, rows, :] = bottom[:, 128:]
                    return carry

                lax.fori_loop(0, 16, place, 0, unroll=4)

    @pl.when(info[3] == 0)
    def _():
        join(mine, theirs)

    @pl.when(info[3] != 0)
    def _():
        join(theirs, mine)


def joined(info, mine, theirs):
    return pl.pallas_call(
        join_kernel,
        in_specs=[pl.BlockSpec(memory_space=pltpu.SMEM)] + [pl.BlockSpec()] * 2,
        out_shape=jax.ShapeDtypeStruct((9, CHANS, CHANS), F32),
        compiler_params=pltpu.CompilerParams(vmem_limit_bytes=32 << 20),
    )(info, mine, theirs)


def edges(first, last):
    n = lax.axis_size("tile")
    above = lax.ppermute(last, "tile", [(i, (i + 1) % n) for i in range(n)])
    below = lax.ppermute(first, "tile", [((i + 1) % n, i) for i in range(n)])
    return above, below


def close_frame(info, window):
    @pl.when(info[4] == 0)
    def _():
        window[:, 0] = jnp.zeros((HERE, COLS, CHANS), BF16)

    @pl.when(info[4] == info[5] - 1)
    def _():
        window[:, ROWS + 1] = jnp.zeros((HERE, COLS, CHANS), BF16)


def on_device(features, conv_weight, codebook, codes, upstream):
    info = place()
    above, below = edges(features[:, :1], features[:, -1:])
    marked, extra = entry_lists(codes)
    grad, grad_first, grad_last, send, keep, weight_send, weight_keep = quantizer(
        marked.reshape(-1), codes.reshape(-1), extra, info, codebook, features, above, below,
        conv_weight, upstream.reshape(SPOTS, CHANS),
    )
    got = lax.ppermute(send, BOTH, SWAP)
    grad4 = grad.reshape(features.shape)
    grad_above, grad_below = edges(grad_first, grad_last)
    weight_got = lax.ppermute(weight_send, BOTH, SWAP)
    weight_chip = (weight_keep.astype(F32) + weight_got.astype(F32)).astype(BF16)
    keep, got, grad_above, grad_below = lax.optimization_barrier(
        (keep, got, grad_above, grad_below)
    )
    weight_ring = weight_chip[0].astype(F32)
    for d in (1, 2, 3):
        weight_ring = weight_ring + lax.ppermute(weight_chip[d], BOTH, first_ring(d)).astype(F32)
    chip = [
        (keep[j].astype(F32) + got[j].astype(F32)).astype(BF16).reshape(16, SHARE, CHANS)
        for j in range(4)
    ]
    others = [lax.ppermute(chip[d], BOTH, first_ring(d)) for d in (1, 2, 3)]
    weight_ring, grad_above = lax.optimization_barrier((weight_ring.astype(BF16), grad_above))
    plane = lax.all_to_all(weight_ring, BOTH, 0, 0, axis_index_groups=PLANES)
    back = feature_grads(info, grad4, grad_above, grad_below, conv_weight)
    piece = plane.astype(F32).sum(0).astype(BF16)
    piece, back = lax.optimization_barrier((piece, back))
    pieces = lax.all_to_all(
        jnp.broadcast_to(piece[None], (16,) + PIECE), BOTH, 0, 0, axis_index_groups=PLANES
    )
    ring = chip[0].astype(F32)
    for other in others:
        ring = ring + other.astype(F32)
    plane = lax.all_to_all(ring.astype(BF16), BOTH, 0, 0, axis_index_groups=PLANES)
    around = [lax.ppermute(pieces, BOTH, first_ring(d)) for d in (1, 2, 3)]
    mine = turned(info, pieces, around)
    theirs = lax.ppermute(mine, BOTH, SWAP)
    code_part = plane.astype(F32).sum(0)
    return back.reshape(features.shape), joined(info, mine, theirs), code_part


def solution(mesh):
    in_specs = (
        P("clip", "tile", None, None),
        P(),
        P(),
        P(None, "clip", "tile", None),
        P("clip", "tile", None, None),
    )
    out_specs = (P("clip", "tile", None, None), P(), P(BOTH, None))
    return jax.shard_map(
        on_device, mesh=mesh, in_specs=in_specs, out_specs=out_specs, check_vma=False
    )
```

```python
import functools

import jax
import jax.numpy as jnp
from jax import lax
from jax.experimental import pallas as pl
from jax.experimental.pallas import tpu as pltpu
from jax.sharding import PartitionSpec as P

BETA = 0.25
BOTH = ("clip", "tile")
F32, BF16 = jnp.float32, jnp.bfloat16

CHANS = 256
CODES = 16384
DEPTHS = 4
COLS = 128
ROWS = 16
HERE = 2
SPOTS = HERE * ROWS * COLS
BLOCK = 4 * COLS
BLOCKS = SPOTS // BLOCK
TALL = 4
GROUP = TALL * DEPTHS
STRIPS = SPOTS // (TALL * COLS)
GROUPS = DEPTHS * SPOTS // GROUP
SPILL = 64
CHUNKS = 8
UNROLL = 16
PIECES = 96
PIECE = (16, 384)
SHARE = CODES // 128


def lin(x, y, z, core):
    return (((z & 1) * 4 + y) * 2 + core) * 8 + x * 2 + (z >> 1)


def moves(where):
    return [
        (lin(x, y, z, c), lin(*where(x, y, z, c)))
        for x in range(4)
        for y in range(4)
        for z in range(4)
        for c in range(2)
    ]


SWAP = moves(lambda x, y, z, c: (x, y, z, 1 - c))


def first_ring(d):
    return moves(lambda x, y, z, c: ((x + d) % 4, y, z, c) if c == 0 else (x, (y + d) % 4, z, c))


PLANES = [[lin(x, y, z, 0) for y in range(4) for z in range(4)] for x in range(4)] + [
    [lin(x, y, z, 1) for x in range(4) for z in range(4)] for y in range(4)
]


def place():
    clip, tile = lax.axis_index("clip"), lax.axis_index("tile")
    core, y, z_lo = clip % 2, (clip // 2) % 4, clip // 8
    x, z_hi = tile // 2, tile % 2
    return jnp.stack([x, y, z_hi * 2 + z_lo, core, tile, lax.axis_size("tile")]).astype(jnp.int32)


def owner(x0, y0, core, j, m):
    other, z = m >> 2, m & 3
    x = jnp.where(core == 0, (x0 + j) & 3, other)
    y = jnp.where(core == 0, other, (y0 + j) & 3)
    return lin(x, y, z, core)


def shifted(value, by):
    n = value.shape[0]
    col = lax.broadcasted_iota(jnp.int32, value.shape, 0) % COLS
    if by == 1:
        return jnp.where(col == 0, 0.0, pltpu.roll(value, 1, axis=0))
    return jnp.where(col == COLS - 1, 0.0, pltpu.roll(value, n - 1, axis=0))


def window_copies(above, mid, below, window, sems, first=0):
    found = []
    for n in range(HERE):
        for source, row, count in ((above, 0, 1), (mid, 1, ROWS), (below, ROWS + 1, 1)):
            found.append(
                pltpu.make_async_copy(
                    source.at[n], window.at[n, pl.ds(row, count)], sems.at[first + len(found)]
                )
            )
    return found


def list_kernel(codes, marked, extra, parts):
    cells = [
        codes[pl.ds(d * HERE * ROWS + r, STRIPS, stride=TALL), :]
        for r in range(TALL)
        for d in range(DEPTHS)
    ]
    later = []
    for a in range(GROUP):
        hit = None
        for b in range(a + 1, GROUP):
            same = (cells[a] == cells[b]).astype(jnp.int32)
            hit = same if hit is None else jnp.maximum(hit, same)
        later.append(jnp.zeros_like(cells[a]) if hit is None else hit)
    flags = jnp.concatenate(later, axis=0)
    entries = jnp.concatenate(cells, axis=0)
    line = lax.broadcasted_iota(jnp.int32, (128, 128), 0)
    lane = lax.broadcasted_iota(jnp.int32, (128, 128), 1)
    bits = flags.astype(F32)
    inside = jnp.dot(bits, (line < lane).astype(F32), preferred_element_type=F32)
    per_row = jnp.dot(bits, jnp.ones((128, 128), F32), preferred_element_type=F32)
    ahead = jnp.dot((lane < line).astype(F32), per_row, preferred_element_type=F32)
    rank = (inside + ahead).astype(jnp.int32)
    marked[...] = 2 * jnp.where(flags > 0, CODES + rank, entries)
    rank = jnp.where(flags > 0, rank, -1)
    for s in range(SPILL):
        parts[pl.ds(s, 1), :] = jnp.sum(
            jnp.where(rank == s, 2 * entries, 0), axis=0, keepdims=True
        )
    codes_of = jnp.sum(parts[...].astype(F32), axis=1, keepdims=True)
    square = lax.broadcasted_iota(jnp.int32, (SPILL, 128), 0) == lax.broadcasted_iota(
        jnp.int32, (SPILL, 128), 1
    )
    spilled = jnp.sum(jnp.where(square, codes_of, 0.0), axis=0, keepdims=True)
    whole = jnp.sum(per_row, axis=0, keepdims=True)
    both = jnp.concatenate([jnp.broadcast_to(spilled, (4, 128)), jnp.broadcast_to(whole, (4, 128))])
    extra[...] = both.astype(jnp.int32)


def entry_lists(codes):
    ints = jnp.int32
    return pl.pallas_call(
        list_kernel,
        out_shape=[
            jax.ShapeDtypeStruct((128, 128), ints),
            jax.ShapeDtypeStruct((8, 128), ints),
        ],
        scratch_shapes=[pltpu.VMEM((SPILL, 128), ints)],
    )(codes.reshape(128, 128))


def quantizer_kernel(
    extra, info,
    marked, plain, codebook, feats, above, below, weights, up,
    grad, grad_first, grad_last, send, keep, weight_send, weight_keep,
    table, sums, lat, raw, near, taps, window, weight_sum, weight_out, all_ids, sems, *ids,
):
    many = extra[4, 0]
    windows = window_copies(above, feats, below, window, sems)
    get_taps = pltpu.make_async_copy(weights, taps, sems.at[6])
    get_ids = [
        pltpu.make_async_copy(marked.at[pl.ds(c * GROUPS, GROUPS)], ids[c], sems.at[26 + c])
        for c in range(GROUP)
    ]
    get_up = pltpu.make_async_copy(up, near, sems.at[8])
    chunk = CODES // CHUNKS

    def get_table(c):
        rows = pl.ds(c * chunk, chunk)
        return pltpu.make_async_copy(codebook.at[rows], raw.at[rows], sems.at[16 + c])

    early = [get_taps] + windows[:3]
    for copy in early + windows[3:]:
        copy.start()
    for copy in early + windows[3:]:
        copy.wait()
    close_frame(info, window)
    for c in range(CHUNKS):
        get_table(c).start()
    for copy in get_ids + [get_up]:
        copy.start()

    def line(block, r):
        return pl.multiple_of(block * (2 * TALL * COLS), 8) + 2 * r

    def convolve(block, carry):
        clip = block >> 2
        row = (block & 3) * 4
        cols = [None] * 3
        for a in range(3):
            part = window[clip, pl.ds(row + a, 4)].reshape(BLOCK, CHANS)
            for b in range(3):
                term = jnp.dot(part, taps[3 * a + b], preferred_element_type=F32)
                cols[b] = term if a == 0 else cols[b] + term
        latent = shifted(cols[0], 1) + cols[1] + shifted(cols[2], -1)
        for r in range(4):
            at = line(block, r)
            own = latent[r * COLS : (r + 1) * COLS]
            lat[pl.ds(at, COLS, stride=2 * TALL), :] = own[:, :128]
            lat[pl.ds(at + 1, COLS, stride=2 * TALL), :] = own[:, 128:]
        return carry

    lax.fori_loop(0, BLOCKS, convolve, 0)

    for c in range(CHUNKS):
        get_table(c).wait()

        def convert(t, carry):
            at = pl.multiple_of(c * chunk + t * 512, 16)
            part = raw[pl.ds(at, 512), :].astype(F32)
            at = pl.multiple_of(2 * at, 8)
            table[pl.ds(at, 512, stride=2), :] = part[:, :128]
            table[pl.ds(at + 1, 512, stride=2), :] = part[:, 128:]
            sums[pl.ds(at, 1024), :] = jnp.zeros((1024, 128), F32)
            return carry

        lax.fori_loop(0, chunk // 512, convert, 0)

    sums[pl.ds(2 * CODES, 2 * SPILL), :] = jnp.zeros((2 * SPILL, 128), F32)

    def lend(s, carry):
        table[pl.ds(2 * (CODES + s), 2), :] = table[pl.ds(extra[0, s], 2), :]
        return carry

    lax.fori_loop(0, jnp.minimum(many, SPILL), lend, 0)

    def resids(group, code):
        found = []
        first = pl.multiple_of(group * (2 * TALL), 8)
        for r in range(TALL):
            here = pl.ds(first + 2 * r, 2)
            resid, total = lat[here, :], None
            for d in range(DEPTHS):
                k = code(r, d)
                resid = resid - table[pl.ds(k, 2), :]
                total = resid if total is None else total + resid
                found.append((k, resid))
            lat[here, :] = total
        return found

    for copy in get_ids:
        copy.wait()

    @pl.when(many <= SPILL)
    def _():
        def blocks(block, carry):
            def step(col, carry):
                first = block * COLS + col
                found = resids(first, lambda r, d: ids[r * DEPTHS + d][first])
                new = [sums[pl.ds(k, 2), :] + v for k, v in found]
                for (k, _), v in zip(found, new):
                    sums[pl.ds(k, 2), :] = v
                return carry

            return lax.fori_loop(0, COLS, step, carry, unroll=UNROLL)

        lax.fori_loop(0, STRIPS, blocks, 0)

        def give_back(s, carry):
            k = extra[0, s]
            sums[pl.ds(k, 2), :] = sums[pl.ds(k, 2), :] + sums[pl.ds(2 * (CODES + s), 2), :]
            return carry

        lax.fori_loop(0, many, give_back, 0)

    @pl.when(many > SPILL)
    def _():
        again = pltpu.make_async_copy(plain, all_ids, sems.at[7])
        again.start()
        again.wait()

        def blocks(block, carry):
            def step(col, carry):
                spot = block * (TALL * COLS) + col
                for k, v in resids(block * COLS + col, lambda r, d: 2 * all_ids[d * SPOTS + spot + r * COLS]):
                    sums[pl.ds(k, 2), :] = sums[pl.ds(k, 2), :] + v
                return carry

            return lax.fori_loop(0, COLS, step, carry)

        lax.fori_loop(0, STRIPS, blocks, 0)

    get_up.wait()

    def put_grad(block):
        rows = pl.ds(pl.multiple_of(block * BLOCK, 16), BLOCK)
        return pltpu.make_async_copy(near.at[rows], grad.at[rows], sems.at[8 + block])

    def gradient(block, carry):
        rows = pl.ds(pl.multiple_of(block * BLOCK, 16), BLOCK)
        halves = [
            jnp.concatenate(
                [lat[pl.ds(line(block, r) + h, COLS, stride=2 * TALL), :] for r in range(4)], axis=0
            )
            for h in range(2)
        ]
        total = jnp.concatenate(halves, axis=1)
        near[rows, :] = (near[rows, :].astype(F32) + 2.0 * BETA * total).astype(BF16)
        put_grad(block).start()
        return carry

    lax.fori_loop(0, BLOCKS, gradient, 0)
    put_edges = []
    for out, row in ((grad_first, 0), (grad_last, ROWS - 1)):
        for n in range(HERE):
            rows = pl.ds((n * ROWS + row) * COLS, COLS)
            put_edges.append(
                pltpu.make_async_copy(
                    near.at[rows], out.at[n, 0], sems.at[26 + GROUP + len(put_edges)]
                )
            )
    for copy in put_edges:
        copy.start()

    def put_out(out, first, j):
        rows = pl.ds((first + j) * 16 * SHARE, 16 * SHARE)
        return pltpu.make_async_copy(raw.at[rows], out.at[j], sems.at[16 + first + j])

    def fill(m, carry, first, core, j):
        at = pl.multiple_of(owner(info[0], info[1], core, j, m) * (2 * SHARE), 8)
        rows = pl.ds(pl.multiple_of(((first + j) * 16 + m) * SHARE, 16), SHARE)
        raw[rows, :128] = (sums[pl.ds(at, SHARE, stride=2), :] * -2.0).astype(BF16)
        raw[rows, 128:] = (sums[pl.ds(at + 1, SHARE, stride=2), :] * -2.0).astype(BF16)
        return carry

    for first, core, out in ((0, 1 - info[3], send), (4, info[3], keep)):
        for j in range(4):
            lax.fori_loop(0, 16, functools.partial(fill, first=first, core=core, j=j), 0, unroll=2)
            put_out(out, first, j).start()

    weight_sum[...] = jnp.zeros_like(weight_sum)

    def weigh(block, carry):
        clip = block // (ROWS // 4)
        row = (block % (ROWS // 4)) * 4
        own = near[pl.ds(pl.multiple_of(block * BLOCK, 16), BLOCK), :]
        mid = own.astype(F32)
        wide = jnp.concatenate(
            [shifted(mid, -1).astype(BF16), own, shifted(mid, 1).astype(BF16)], axis=1
        )
        for a in range(3):
            part = window[clip, pl.ds(row + a, 4)].reshape(BLOCK, CHANS)
            weight_sum[pl.ds(a * CHANS, CHANS), :] += lax.dot_general(
                part, wide, (((0,), (0,)), ((), ())), preferred_element_type=F32
            )
        return carry

    lax.fori_loop(0, BLOCKS, weigh, 0)

    def cut(side, core, j):
        ring = (jnp.where(core == 0, info[0], info[1]) + j) % 4
        first = pl.multiple_of(jnp.minimum(core * 64 + ring * 16, PIECES - 16) * 8, 128)
        for m in range(16):
            rows = weight_sum[pl.ds(first + 8 * m, 8), :]
            both = jnp.concatenate([rows[:, :384], rows[:, 384:]], axis=0)
            weight_out[side, j, m] = both.astype(BF16)

    def put_weights(out, side):
        return pltpu.make_async_copy(weight_out.at[side], out, sems.at[24 + side])

    for side, core, out in ((0, 1 - info[3], weight_send), (1, info[3], weight_keep)):
        for j in range(4):
            cut(side, core, j)
        put_weights(out, side).start()
    for copy in put_edges:
        copy.wait()
    for block in range(BLOCKS):
        put_grad(block).wait()
    for first, out in ((0, send), (4, keep)):
        for j in range(4):
            put_out(out, first, j).wait()
    put_weights(weight_send, 0).wait()
    put_weights(weight_keep, 1).wait()


def quantizer(marked, plain, extra, info, codebook, feats, above, below, weights, up):
    hbm = pl.BlockSpec(memory_space=pl.ANY)
    smem = pl.BlockSpec(memory_space=pltpu.SMEM)
    vmem = pl.BlockSpec(memory_space=pltpu.VMEM)
    out_shape = (4, 16 * SHARE, CHANS)
    weight_shape = (4, 16) + PIECE
    return pl.pallas_call(
        quantizer_kernel,
        in_specs=[smem] * 2 + [hbm] * 4 + [vmem] * 2 + [hbm] * 2,
        out_specs=[hbm] * 7,
        scratch_shapes=[
            pltpu.VMEM((2 * (CODES + SPILL), 128), F32),
            pltpu.VMEM((2 * (CODES + SPILL), 128), F32),
            pltpu.VMEM((2 * SPOTS, 128), F32),
            pltpu.VMEM((CODES, CHANS), BF16),
            pltpu.VMEM((SPOTS, CHANS), BF16),
            pltpu.VMEM((9, CHANS, CHANS), BF16),
            pltpu.VMEM((HERE, ROWS + 2, COLS, CHANS), BF16),
            pltpu.VMEM((3 * CHANS, 3 * CHANS), F32),
            pltpu.VMEM((2,) + weight_shape, BF16),
            pltpu.SMEM((DEPTHS * SPOTS,), jnp.int32),
            pltpu.SemaphoreType.DMA((26 + GROUP + 2 * HERE,)),
        ]
        + [pltpu.SMEM((GROUPS,), jnp.int32)] * GROUP,
        out_shape=[
            jax.ShapeDtypeStruct((SPOTS, CHANS), BF16),
            jax.ShapeDtypeStruct((HERE, 1, COLS, CHANS), BF16),
            jax.ShapeDtypeStruct((HERE, 1, COLS, CHANS), BF16),
            jax.ShapeDtypeStruct(out_shape, BF16),
            jax.ShapeDtypeStruct(out_shape, BF16),
            jax.ShapeDtypeStruct(weight_shape, BF16),
            jax.ShapeDtypeStruct(weight_shape, BF16),
        ],
        compiler_params=pltpu.CompilerParams(vmem_limit_bytes=58 << 20),
        cost_estimate=pl.CostEstimate(
            flops=4 * 9 * SPOTS * CHANS * CHANS, bytes_accessed=64 << 20, transcendentals=0
        ),
    )(extra, info, marked, plain, codebook, feats, above, below, weights, up)


def back_kernel(info, grad, above, below, weights, out, window, sems):
    i = pl.program_id(0)

    copies = window_copies(above, grad, below, window, sems)

    @pl.when(i == 0)
    def _():
        for copy in copies:
            copy.start()
        for copy in copies:
            copy.wait()
        close_frame(info, window)

    clip = i // (ROWS // 4)
    row = (i % (ROWS // 4)) * 4
    cols = [None] * 3
    for a in range(3):
        part = window[clip, pl.ds(row + 2 - a, 4)].reshape(BLOCK, CHANS)
        for b in range(3):
            term = lax.dot_general(
                part, weights[3 * a + b], (((1,), (1,)), ((), ())), preferred_element_type=F32
            )
            cols[b] = term if a == 0 else cols[b] + term
    back = shifted(cols[0], -1) + cols[1] + shifted(cols[2], 1)
    out[...] = back.astype(BF16)


def feature_grads(info, grad, above, below, weights):
    return pl.pallas_call(
        back_kernel,
        grid=(BLOCKS,),
        in_specs=[
            pl.BlockSpec(memory_space=pltpu.SMEM),
            pl.BlockSpec(memory_space=pl.ANY),
            pl.BlockSpec(memory_space=pl.ANY),
            pl.BlockSpec(memory_space=pl.ANY),
            pl.BlockSpec((9, CHANS, CHANS), lambda i: (0, 0, 0)),
        ],
        out_specs=pl.BlockSpec((BLOCK, CHANS), lambda i: (i, 0)),
        scratch_shapes=[
            pltpu.VMEM((HERE, ROWS + 2, COLS, CHANS), BF16),
            pltpu.SemaphoreType.DMA((3 * HERE,)),
        ],
        out_shape=jax.ShapeDtypeStruct((SPOTS, CHANS), BF16),
        compiler_params=pltpu.CompilerParams(
            vmem_limit_bytes=32 << 20, dimension_semantics=("arbitrary",)
        ),
        cost_estimate=pl.CostEstimate(
            flops=2 * 9 * SPOTS * CHANS * CHANS, bytes_accessed=8 << 20, transcendentals=0
        ),
    )(info, grad, above, below, weights)


def add_kernel(*refs):
    *parts, out = refs
    rows = 256

    def add(i, carry):
        here = pl.ds(pl.multiple_of(i * rows, 16), rows)
        total = parts[0][here, :].astype(F32)
        for part in parts[1:]:
            total = total + part[here, :].astype(F32)
        out[here, :] = total.astype(BF16)
        return carry

    lax.fori_loop(0, out.shape[0] // rows, add, 0)


def added(*parts):
    shape = parts[0].shape
    flat = [part.reshape(-1, CHANS) for part in parts]
    total = pl.pallas_call(
        add_kernel,
        out_shape=jax.ShapeDtypeStruct(flat[0].shape, BF16),
        compiler_params=pltpu.CompilerParams(vmem_limit_bytes=24 << 20),
        cost_estimate=pl.CostEstimate(
            flops=2 * flat[0].size, bytes_accessed=8 * flat[0].size, transcendentals=0
        ),
    )(*flat)
    return total.reshape(shape)


def turn_kernel(info, *refs):
    at = jnp.where(info[3] == 0, info[0], info[1])
    for d in range(4):
        refs[4][(at + 4 - d) % 4] = refs[d][...]


def turned(info, pieces, around):
    return pl.pallas_call(
        turn_kernel,
        in_specs=[pl.BlockSpec(memory_space=pltpu.SMEM)] + [pl.BlockSpec()] * 4,
        out_shape=jax.ShapeDtypeStruct((4,) + pieces.shape, BF16),
    )(info, pieces, *around)


def join_kernel(info, mine, theirs, out):
    def join(low, high):
        for a in range(3):
            for r in range(2):

                def place(m, carry):
                    ref, ring = (low, 2 * a + r) if a < 2 else (high, r)
                    both = ref[ring, m].astype(F32)
                    top, bottom = both[:8], both[8:]
                    rows = pl.ds(pl.multiple_of((r * 16 + m) * 8, 8), 8)
                    out[3 * a, rows, :] = top[:, :256]
                    out[3 * a + 1, rows, :128] = top[:, 256:]
                    out[3 * a + 1, rows, 128:] = bottom[:, :128]
                    out[3 * a + 2, rows, :] = bottom[:, 128:]
                    return carry

                lax.fori_loop(0, 16, place, 0, unroll=4)

    @pl.when(info[3] == 0)
    def _():
        join(mine, theirs)

    @pl.when(info[3] != 0)
    def _():
        join(theirs, mine)


def joined(info, mine, theirs):
    return pl.pallas_call(
        join_kernel,
        in_specs=[pl.BlockSpec(memory_space=pltpu.SMEM)] + [pl.BlockSpec()] * 2,
        out_shape=jax.ShapeDtypeStruct((9, CHANS, CHANS), F32),
        compiler_params=pltpu.CompilerParams(vmem_limit_bytes=32 << 20),
    )(info, mine, theirs)


def edges(first, last):
    n = lax.axis_size("tile")
    above = lax.ppermute(last, "tile", [(i, (i + 1) % n) for i in range(n)])
    below = lax.ppermute(first, "tile", [((i + 1) % n, i) for i in range(n)])
    return above, below


def close_frame(info, window):
    @pl.when(info[4] == 0)
    def _():
        window[:, 0] = jnp.zeros((HERE, COLS, CHANS), BF16)

    @pl.when(info[4] == info[5] - 1)
    def _():
        window[:, ROWS + 1] = jnp.zeros((HERE, COLS, CHANS), BF16)


def on_device(features, conv_weight, codebook, codes, upstream):
    info = place()
    above, below = edges(features[:, :1], features[:, -1:])
    marked, extra = entry_lists(codes)
    grad, grad_first, grad_last, send, keep, weight_send, weight_keep = quantizer(
        marked.reshape(-1), codes.reshape(-1), extra, info, codebook, features, above, below,
        conv_weight, upstream.reshape(SPOTS, CHANS),
    )
    got = lax.ppermute(send, BOTH, SWAP)
    grad4 = grad.reshape(features.shape)
    grad_above, grad_below = edges(grad_first, grad_last)
    weight_got = lax.ppermute(weight_send, BOTH, SWAP)
    weight_chip = (weight_keep.astype(F32) + weight_got.astype(F32)).astype(BF16)
    keep, got, grad_above, grad_below = lax.optimization_barrier(
        (keep, got, grad_above, grad_below)
    )
    weight_ring = weight_chip[0].astype(F32)
    for d in (1, 2, 3):
        weight_ring = weight_ring + lax.ppermute(weight_chip[d], BOTH, first_ring(d)).astype(F32)
    chip = [
        (keep[j].astype(F32) + got[j].astype(F32)).astype(BF16).reshape(16, SHARE, CHANS)
        for j in range(4)
    ]
    others = [lax.ppermute(chip[d], BOTH, first_ring(d)) for d in (1, 2, 3)]
    weight_ring, grad_above = lax.optimization_barrier((weight_ring.astype(BF16), grad_above))
    plane = lax.all_to_all(weight_ring, BOTH, 0, 0, axis_index_groups=PLANES)
    back = feature_grads(info, grad4, grad_above, grad_below, conv_weight)
    piece = plane.astype(F32).sum(0).astype(BF16)
    piece, back = lax.optimization_barrier((piece, back))
    pieces = lax.all_to_all(
        jnp.broadcast_to(piece[None], (16,) + PIECE), BOTH, 0, 0, axis_index_groups=PLANES
    )
    ring = added(chip[0], *others)
    plane = lax.all_to_all(ring, BOTH, 0, 0, axis_index_groups=PLANES)
    around = [lax.ppermute(pieces, BOTH, first_ring(d)) for d in (1, 2, 3)]
    mine = turned(info, pieces, around)
    theirs = lax.ppermute(mine, BOTH, SWAP)
    code_part = plane.astype(F32).sum(0)
    return back.reshape(features.shape), joined(info, mine, theirs), code_part


def solution(mesh):
    in_specs = (
        P("clip", "tile", None, None),
        P(),
        P(),
        P(None, "clip", "tile", None),
        P("clip", "tile", None, None),
    )
    out_specs = (P("clip", "tile", None, None), P(), P(BOTH, None))
    return jax.shard_map(
        on_device, mesh=mesh, in_specs=in_specs, out_specs=out_specs, check_vma=False
    )
```

```python
import functools

import jax
import jax.numpy as jnp
from jax import lax
from jax.experimental import pallas as pl
from jax.experimental.pallas import tpu as pltpu
from jax.sharding import PartitionSpec as P

BETA = 0.25
BOTH = ("clip", "tile")
F32, BF16 = jnp.float32, jnp.bfloat16

CHANS = 256
CODES = 16384
DEPTHS = 4
COLS = 128
ROWS = 16
HERE = 2
SPOTS = HERE * ROWS * COLS
BLOCK = 4 * COLS
BLOCKS = SPOTS // BLOCK
TALL = 4
GROUP = TALL * DEPTHS
STRIPS = SPOTS // (TALL * COLS)
GROUPS = DEPTHS * SPOTS // GROUP
SPILL = 64
CHUNKS = 8
UNROLL = 16
PIECES = 96
PIECE = (16, 384)
SHARE = CODES // 128


def lin(x, y, z, core):
    return (((z & 1) * 4 + y) * 2 + core) * 8 + x * 2 + (z >> 1)


def moves(where):
    return [
        (lin(x, y, z, c), lin(*where(x, y, z, c)))
        for x in range(4)
        for y in range(4)
        for z in range(4)
        for c in range(2)
    ]


SWAP = moves(lambda x, y, z, c: (x, y, z, 1 - c))


def first_ring(d):
    return moves(lambda x, y, z, c: ((x + d) % 4, y, z, c) if c == 0 else (x, (y + d) % 4, z, c))


PLANES = [[lin(x, y, z, 0) for y in range(4) for z in range(4)] for x in range(4)] + [
    [lin(x, y, z, 1) for x in range(4) for z in range(4)] for y in range(4)
]


def place():
    clip, tile = lax.axis_index("clip"), lax.axis_index("tile")
    core, y, z_lo = clip % 2, (clip // 2) % 4, clip // 8
    x, z_hi = tile // 2, tile % 2
    return jnp.stack([x, y, z_hi * 2 + z_lo, core, tile, lax.axis_size("tile")]).astype(jnp.int32)


def owner(x0, y0, core, j, m):
    other, z = m >> 2, m & 3
    x = jnp.where(core == 0, (x0 + j) & 3, other)
    y = jnp.where(core == 0, other, (y0 + j) & 3)
    return lin(x, y, z, core)


def shifted(value, by):
    n = value.shape[0]
    col = lax.broadcasted_iota(jnp.int32, value.shape, 0) % COLS
    if by == 1:
        return jnp.where(col == 0, 0.0, pltpu.roll(value, 1, axis=0))
    return jnp.where(col == COLS - 1, 0.0, pltpu.roll(value, n - 1, axis=0))


def window_copies(above, mid, below, window, sems, first=0):
    found = []
    for n in range(HERE):
        for source, row, count in ((above, 0, 1), (mid, 1, ROWS), (below, ROWS + 1, 1)):
            found.append(
                pltpu.make_async_copy(
                    source.at[n], window.at[n, pl.ds(row, count)], sems.at[first + len(found)]
                )
            )
    return found


def list_kernel(codes, marked, extra, parts):
    cells = [
        codes[pl.ds(d * HERE * ROWS + r, STRIPS, stride=TALL), :]
        for r in range(TALL)
        for d in range(DEPTHS)
    ]
    later = []
    for a in range(GROUP):
        hit = None
        for b in range(a + 1, GROUP):
            same = (cells[a] == cells[b]).astype(jnp.int32)
            hit = same if hit is None else jnp.maximum(hit, same)
        later.append(jnp.zeros_like(cells[a]) if hit is None else hit)
    flags = jnp.concatenate(later, axis=0)
    entries = jnp.concatenate(cells, axis=0)
    line = lax.broadcasted_iota(jnp.int32, (128, 128), 0)
    lane = lax.broadcasted_iota(jnp.int32, (128, 128), 1)
    bits = flags.astype(F32)
    inside = jnp.dot(bits, (line < lane).astype(F32), preferred_element_type=F32)
    per_row = jnp.dot(bits, jnp.ones((128, 128), F32), preferred_element_type=F32)
    ahead = jnp.dot((lane < line).astype(F32), per_row, preferred_element_type=F32)
    rank = (inside + ahead).astype(jnp.int32)
    marked[...] = 2 * jnp.where(flags > 0, CODES + rank, entries)
    rank = jnp.where(flags > 0, rank, -1)
    for s in range(SPILL):
        parts[pl.ds(s, 1), :] = jnp.sum(
            jnp.where(rank == s, 2 * entries, 0), axis=0, keepdims=True
        )
    codes_of = jnp.sum(parts[pl.ds(0, SPILL), :].astype(F32), axis=1, keepdims=True)
    square = lax.broadcasted_iota(jnp.int32, (SPILL, 128), 0) == lax.broadcasted_iota(
        jnp.int32, (SPILL, 128), 1
    )
    spilled = jnp.sum(jnp.where(square, codes_of, 0.0), axis=0, keepdims=True)
    whole = jnp.sum(per_row, axis=0, keepdims=True)
    both = jnp.concatenate([jnp.broadcast_to(spilled, (4, 128)), jnp.broadcast_to(whole, (4, 128))])
    extra[...] = both.astype(jnp.int32)


def entry_lists(codes):
    ints = jnp.int32
    return pl.pallas_call(
        list_kernel,
        out_shape=[
            jax.ShapeDtypeStruct((128, 128), ints),
            jax.ShapeDtypeStruct((8, 128), ints),
        ],
        scratch_shapes=[pltpu.VMEM((SPILL + 8, 128), ints)],
    )(codes.reshape(128, 128))


def quantizer_kernel(
    extra, info,
    marked, plain, codebook, feats, above, below, weights, up,
    grad, grad_first, grad_last, send, keep, weight_send, weight_keep,
    table, sums, lat, raw, near, taps, window, weight_sum, weight_out, all_ids, sems, *ids,
):
    many = extra[4, 0]
    windows = window_copies(above, feats, below, window, sems)
    get_taps = pltpu.make_async_copy(weights, taps, sems.at[6])
    get_ids = [
        pltpu.make_async_copy(marked.at[pl.ds(c * GROUPS, GROUPS)], ids[c], sems.at[26 + c])
        for c in range(GROUP)
    ]
    get_up = pltpu.make_async_copy(up, near, sems.at[8])
    chunk = CODES // CHUNKS

    def get_table(c):
        rows = pl.ds(c * chunk, chunk)
        return pltpu.make_async_copy(codebook.at[rows], raw.at[rows], sems.at[16 + c])

    early = [get_taps] + windows[:3]
    for copy in early + windows[3:]:
        copy.start()
    for copy in early + windows[3:]:
        copy.wait()
    close_frame(info, window)
    for c in range(CHUNKS):
        get_table(c).start()
    for copy in get_ids + [get_up]:
        copy.start()

    def line(block, r):
        return pl.multiple_of(block * (2 * TALL * COLS), 8) + 2 * r

    def convolve(block, carry):
        clip = block >> 2
        row = (block & 3) * 4
        cols = [None] * 3
        for a in range(3):
            part = window[clip, pl.ds(row + a, 4)].reshape(BLOCK, CHANS)
            for b in range(3):
                term = jnp.dot(part, taps[3 * a + b], preferred_element_type=F32)
                cols[b] = term if a == 0 else cols[b] + term
        latent = shifted(cols[0], 1) + cols[1] + shifted(cols[2], -1)
        for r in range(4):
            at = line(block, r)
            own = latent[r * COLS : (r + 1) * COLS]
            lat[pl.ds(at, COLS, stride=2 * TALL), :] = own[:, :128]
            lat[pl.ds(at + 1, COLS, stride=2 * TALL), :] = own[:, 128:]
        return carry

    lax.fori_loop(0, BLOCKS, convolve, 0)

    for c in range(CHUNKS):
        get_table(c).wait()

        def convert(t, carry):
            at = pl.multiple_of(c * chunk + t * 512, 16)
            part = raw[pl.ds(at, 512), :].astype(F32)
            at = pl.multiple_of(2 * at, 8)
            table[pl.ds(at, 512, stride=2), :] = part[:, :128]
            table[pl.ds(at + 1, 512, stride=2), :] = part[:, 128:]
            sums[pl.ds(at, 1024), :] = jnp.zeros((1024, 128), F32)
            return carry

        lax.fori_loop(0, chunk // 512, convert, 0)

    sums[pl.ds(2 * CODES, 2 * SPILL), :] = jnp.zeros((2 * SPILL, 128), F32)

    def lend(s, carry):
        table[pl.ds(2 * (CODES + s), 2), :] = table[pl.ds(extra[0, s], 2), :]
        return carry

    lax.fori_loop(0, jnp.minimum(many, SPILL), lend, 0)

    def resids(group, code):
        found = []
        first = pl.multiple_of(group * (2 * TALL), 8)
        for r in range(TALL):
            here = pl.ds(first + 2 * r, 2)
            resid, total = lat[here, :], None
            for d in range(DEPTHS):
                k = code(r, d)
                resid = resid - table[pl.ds(k, 2), :]
                total = resid if total is None else total + resid
                found.append((k, resid))
            lat[here, :] = total
        return found

    for copy in get_ids:
        copy.wait()

    @pl.when(many <= SPILL)
    def _():
        def blocks(block, carry):
            def step(col, carry):
                first = block * COLS + col
                found = resids(first, lambda r, d: ids[r * DEPTHS + d][first])
                new = [sums[pl.ds(k, 2), :] + v for k, v in found]
                for (k, _), v in zip(found, new):
                    sums[pl.ds(k, 2), :] = v
                return carry

            return lax.fori_loop(0, COLS, step, carry, unroll=UNROLL)

        lax.fori_loop(0, STRIPS, blocks, 0)

        def give_back(s, carry):
            k = extra[0, s]
            sums[pl.ds(k, 2), :] = sums[pl.ds(k, 2), :] + sums[pl.ds(2 * (CODES + s), 2), :]
            return carry

        lax.fori_loop(0, many, give_back, 0)

    @pl.when(many > SPILL)
    def _():
        again = pltpu.make_async_copy(plain, all_ids, sems.at[7])
        again.start()
        again.wait()

        def blocks(block, carry):
            def step(col, carry):
                spot = block * (TALL * COLS) + col
                for k, v in resids(block * COLS + col, lambda r, d: 2 * all_ids[d * SPOTS + spot + r * COLS]):
                    sums[pl.ds(k, 2), :] = sums[pl.ds(k, 2), :] + v
                return carry

            return lax.fori_loop(0, COLS, step, carry)

        lax.fori_loop(0, STRIPS, blocks, 0)

    get_up.wait()

    def put_grad(block):
        rows = pl.ds(pl.multiple_of(block * BLOCK, 16), BLOCK)
        return pltpu.make_async_copy(near.at[rows], grad.at[rows], sems.at[8 + block])

    def gradient(block, carry):
        rows = pl.ds(pl.multiple_of(block * BLOCK, 16), BLOCK)
        halves = [
            jnp.concatenate(
                [lat[pl.ds(line(block, r) + h, COLS, stride=2 * TALL), :] for r in range(4)], axis=0
            )
            for h in range(2)
        ]
        total = jnp.concatenate(halves, axis=1)
        near[rows, :] = (near[rows, :].astype(F32) + 2.0 * BETA * total).astype(BF16)
        put_grad(block).start()
        return carry

    lax.fori_loop(0, BLOCKS, gradient, 0)
    put_edges = []
    for out, row in ((grad_first, 0), (grad_last, ROWS - 1)):
        for n in range(HERE):
            rows = pl.ds((n * ROWS + row) * COLS, COLS)
            put_edges.append(
                pltpu.make_async_copy(
                    near.at[rows], out.at[n, 0], sems.at[26 + GROUP + len(put_edges)]
                )
            )
    for copy in put_edges:
        copy.start()

    def put_out(out, first, j):
        rows = pl.ds((first + j) * 16 * SHARE, 16 * SHARE)
        return pltpu.make_async_copy(raw.at[rows], out.at[j], sems.at[16 + first + j])

    def fill(m, carry, first, core, j):
        at = pl.multiple_of(owner(info[0], info[1], core, j, m) * (2 * SHARE), 8)
        rows = pl.ds(pl.multiple_of(((first + j) * 16 + m) * SHARE, 16), SHARE)
        raw[rows, :128] = (sums[pl.ds(at, SHARE, stride=2), :] * -2.0).astype(BF16)
        raw[rows, 128:] = (sums[pl.ds(at + 1, SHARE, stride=2), :] * -2.0).astype(BF16)
        return carry

    for first, core, out in ((0, 1 - info[3], send), (4, info[3], keep)):
        for j in range(4):
            lax.fori_loop(0, 16, functools.partial(fill, first=first, core=core, j=j), 0, unroll=2)
            put_out(out, first, j).start()

    weight_sum[...] = jnp.zeros_like(weight_sum)

    def weigh(block, carry):
        clip = block // (ROWS // 4)
        row = (block % (ROWS // 4)) * 4
        own = near[pl.ds(pl.multiple_of(block * BLOCK, 16), BLOCK), :]
        mid = own.astype(F32)
        wide = jnp.concatenate(
            [shifted(mid, -1).astype(BF16), own, shifted(mid, 1).astype(BF16)], axis=1
        )
        for a in range(3):
            part = window[clip, pl.ds(row + a, 4)].reshape(BLOCK, CHANS)
            weight_sum[pl.ds(a * CHANS, CHANS), :] += lax.dot_general(
                part, wide, (((0,), (0,)), ((), ())), preferred_element_type=F32
            )
        return carry

    lax.fori_loop(0, BLOCKS, weigh, 0)

    def cut(side, core, j):
        ring = (jnp.where(core == 0, info[0], info[1]) + j) % 4
        first = pl.multiple_of(jnp.minimum(core * 64 + ring * 16, PIECES - 16) * 8, 128)
        for m in range(16):
            rows = weight_sum[pl.ds(first + 8 * m, 8), :]
            both = jnp.concatenate([rows[:, :384], rows[:, 384:]], axis=0)
            weight_out[side, j, m] = both.astype(BF16)

    def put_weights(out, side):
        return pltpu.make_async_copy(weight_out.at[side], out, sems.at[24 + side])

    for side, core, out in ((0, 1 - info[3], weight_send), (1, info[3], weight_keep)):
        for j in range(4):
            cut(side, core, j)
        put_weights(out, side).start()
    for copy in put_edges:
        copy.wait()
    for block in range(BLOCKS):
        put_grad(block).wait()
    for first, out in ((0, send), (4, keep)):
        for j in range(4):
            put_out(out, first, j).wait()
    put_weights(weight_send, 0).wait()
    put_weights(weight_keep, 1).wait()


def quantizer(marked, plain, extra, info, codebook, feats, above, below, weights, up):
    hbm = pl.BlockSpec(memory_space=pl.ANY)
    smem = pl.BlockSpec(memory_space=pltpu.SMEM)
    vmem = pl.BlockSpec(memory_space=pltpu.VMEM)
    out_shape = (4, 16 * SHARE, CHANS)
    weight_shape = (4, 16) + PIECE
    return pl.pallas_call(
        quantizer_kernel,
        in_specs=[smem] * 2 + [hbm] * 4 + [vmem] * 2 + [hbm] * 2,
        out_specs=[hbm] * 7,
        scratch_shapes=[
            pltpu.VMEM((2 * (CODES + SPILL) + 8, 128), F32),
            pltpu.VMEM((2 * (CODES + SPILL) + 8, 128), F32),
            pltpu.VMEM((2 * SPOTS + 8, 128), F32),
            pltpu.VMEM((CODES, CHANS), BF16),
            pltpu.VMEM((SPOTS, CHANS), BF16),
            pltpu.VMEM((9, CHANS, CHANS), BF16),
            pltpu.VMEM((HERE, ROWS + 2, COLS, CHANS), BF16),
            pltpu.VMEM((3 * CHANS, 3 * CHANS), F32),
            pltpu.VMEM((2,) + weight_shape, BF16),
            pltpu.SMEM((DEPTHS * SPOTS,), jnp.int32),
            pltpu.SemaphoreType.DMA((26 + GROUP + 2 * HERE,)),
        ]
        + [pltpu.SMEM((GROUPS,), jnp.int32)] * GROUP,
        out_shape=[
            jax.ShapeDtypeStruct((SPOTS, CHANS), BF16),
            jax.ShapeDtypeStruct((HERE, 1, COLS, CHANS), BF16),
            jax.ShapeDtypeStruct((HERE, 1, COLS, CHANS), BF16),
            jax.ShapeDtypeStruct(out_shape, BF16),
            jax.ShapeDtypeStruct(out_shape, BF16),
            jax.ShapeDtypeStruct(weight_shape, BF16),
            jax.ShapeDtypeStruct(weight_shape, BF16),
        ],
        compiler_params=pltpu.CompilerParams(vmem_limit_bytes=58 << 20),
        cost_estimate=pl.CostEstimate(
            flops=4 * 9 * SPOTS * CHANS * CHANS, bytes_accessed=64 << 20, transcendentals=0
        ),
    )(extra, info, marked, plain, codebook, feats, above, below, weights, up)


def back_kernel(info, grad, above, below, weights, out, window, sems):
    i = pl.program_id(0)

    copies = window_copies(above, grad, below, window, sems)

    @pl.when(i == 0)
    def _():
        for copy in copies:
            copy.start()
        for copy in copies:
            copy.wait()
        close_frame(info, window)

    clip = i // (ROWS // 4)
    row = (i % (ROWS // 4)) * 4
    cols = [None] * 3
    for a in range(3):
        part = window[clip, pl.ds(row + 2 - a, 4)].reshape(BLOCK, CHANS)
        for b in range(3):
            term = lax.dot_general(
                part, weights[3 * a + b], (((1,), (1,)), ((), ())), preferred_element_type=F32
            )
            cols[b] = term if a == 0 else cols[b] + term
    back = shifted(cols[0], -1) + cols[1] + shifted(cols[2], 1)
    out[...] = back.astype(BF16)


def feature_grads(info, grad, above, below, weights):
    return pl.pallas_call(
        back_kernel,
        grid=(BLOCKS,),
        in_specs=[
            pl.BlockSpec(memory_space=pltpu.SMEM),
            pl.BlockSpec(memory_space=pl.ANY),
            pl.BlockSpec(memory_space=pl.ANY),
            pl.BlockSpec(memory_space=pl.ANY),
            pl.BlockSpec((9, CHANS, CHANS), lambda i: (0, 0, 0)),
        ],
        out_specs=pl.BlockSpec((BLOCK, CHANS), lambda i: (i, 0)),
        scratch_shapes=[
            pltpu.VMEM((HERE, ROWS + 2, COLS, CHANS), BF16),
            pltpu.SemaphoreType.DMA((3 * HERE,)),
        ],
        out_shape=jax.ShapeDtypeStruct((SPOTS, CHANS), BF16),
        compiler_params=pltpu.CompilerParams(
            vmem_limit_bytes=32 << 20, dimension_semantics=("arbitrary",)
        ),
        cost_estimate=pl.CostEstimate(
            flops=2 * 9 * SPOTS * CHANS * CHANS, bytes_accessed=8 << 20, transcendentals=0
        ),
    )(info, grad, above, below, weights)


def add_kernel(*refs):
    *parts, out = refs
    rows = 256

    def add(i, carry):
        here = pl.ds(pl.multiple_of(i * rows, 16), rows)
        total = parts[0][here, :].astype(F32)
        for part in parts[1:]:
            total = total + part[here, :].astype(F32)
        out[here, :] = total.astype(BF16)
        return carry

    lax.fori_loop(0, out.shape[0] // rows, add, 0)


def added(*parts):
    shape = parts[0].shape
    flat = [part.reshape(-1, CHANS) for part in parts]
    total = pl.pallas_call(
        add_kernel,
        out_shape=jax.ShapeDtypeStruct(flat[0].shape, BF16),
        compiler_params=pltpu.CompilerParams(vmem_limit_bytes=24 << 20),
        cost_estimate=pl.CostEstimate(
            flops=2 * flat[0].size, bytes_accessed=8 * flat[0].size, transcendentals=0
        ),
    )(*flat)
    return total.reshape(shape)


def turn_kernel(info, *refs):
    at = jnp.where(info[3] == 0, info[0], info[1])
    for d in range(4):
        refs[4][(at + 4 - d) % 4] = refs[d][...]


def turned(info, pieces, around):
    return pl.pallas_call(
        turn_kernel,
        in_specs=[pl.BlockSpec(memory_space=pltpu.SMEM)] + [pl.BlockSpec()] * 4,
        out_shape=jax.ShapeDtypeStruct((4,) + pieces.shape, BF16),
    )(info, pieces, *around)


def join_kernel(info, mine, theirs, out):
    def join(low, high):
        for a in range(3):
            for r in range(2):

                def place(m, carry):
                    ref, ring = (low, 2 * a + r) if a < 2 else (high, r)
                    both = ref[ring, m].astype(F32)
                    top, bottom = both[:8], both[8:]
                    rows = pl.ds(pl.multiple_of((r * 16 + m) * 8, 8), 8)
                    out[3 * a, rows, :] = top[:, :256]
                    out[3 * a + 1, rows, :128] = top[:, 256:]
                    out[3 * a + 1, rows, 128:] = bottom[:, :128]
                    out[3 * a + 2, rows, :] = bottom[:, 128:]
                    return carry

                lax.fori_loop(0, 16, place, 0, unroll=4)

    @pl.when(info[3] == 0)
    def _():
        join(mine, theirs)

    @pl.when(info[3] != 0)
    def _():
        join(theirs, mine)


def joined(info, mine, theirs):
    return pl.pallas_call(
        join_kernel,
        in_specs=[pl.BlockSpec(memory_space=pltpu.SMEM)] + [pl.BlockSpec()] * 2,
        out_shape=jax.ShapeDtypeStruct((9, CHANS, CHANS), F32),
        compiler_params=pltpu.CompilerParams(vmem_limit_bytes=32 << 20),
    )(info, mine, theirs)


def edges(first, last):
    n = lax.axis_size("tile")
    above = lax.ppermute(last, "tile", [(i, (i + 1) % n) for i in range(n)])
    below = lax.ppermute(first, "tile", [((i + 1) % n, i) for i in range(n)])
    return above, below


def close_frame(info, window):
    @pl.when(info[4] == 0)
    def _():
        window[:, 0] = jnp.zeros((HERE, COLS, CHANS), BF16)

    @pl.when(info[4] == info[5] - 1)
    def _():
        window[:, ROWS + 1] = jnp.zeros((HERE, COLS, CHANS), BF16)


def on_device(features, conv_weight, codebook, codes, upstream):
    info = place()
    above, below = edges(features[:, :1], features[:, -1:])
    marked, extra = entry_lists(codes)
    grad, grad_first, grad_last, send, keep, weight_send, weight_keep = quantizer(
        marked.reshape(-1), codes.reshape(-1), extra, info, codebook, features, above, below,
        conv_weight, upstream.reshape(SPOTS, CHANS),
    )
    got = lax.ppermute(send, BOTH, SWAP)
    grad4 = grad.reshape(features.shape)
    grad_above, grad_below = edges(grad_first, grad_last)
    weight_got = lax.ppermute(weight_send, BOTH, SWAP)
    weight_chip = (weight_keep.astype(F32) + weight_got.astype(F32)).astype(BF16)
    keep, got, grad_above, grad_below = lax.optimization_barrier(
        (keep, got, grad_above, grad_below)
    )
    weight_ring = weight_chip[0].astype(F32)
    for d in (1, 2, 3):
        weight_ring = weight_ring + lax.ppermute(weight_chip[d], BOTH, first_ring(d)).astype(F32)
    chip = [
        (keep[j].astype(F32) + got[j].astype(F32)).astype(BF16).reshape(16, SHARE, CHANS)
        for j in range(4)
    ]
    others = [lax.ppermute(chip[d], BOTH, first_ring(d)) for d in (1, 2, 3)]
    weight_ring, grad_above = lax.optimization_barrier((weight_ring.astype(BF16), grad_above))
    plane = lax.all_to_all(weight_ring, BOTH, 0, 0, axis_index_groups=PLANES)
    back = feature_grads(info, grad4, grad_above, grad_below, conv_weight)
    piece = plane.astype(F32).sum(0).astype(BF16)
    piece, back = lax.optimization_barrier((piece, back))
    pieces = lax.all_to_all(
        jnp.broadcast_to(piece[None], (16,) + PIECE), BOTH, 0, 0, axis_index_groups=PLANES
    )
    ring = added(chip[0], *others)
    pieces, ring = lax.optimization_barrier((pieces, ring))
    plane = lax.all_to_all(ring, BOTH, 0, 0, axis_index_groups=PLANES)
    around = [lax.ppermute(pieces, BOTH, first_ring(d)) for d in (1, 2, 3)]
    mine = turned(info, pieces, around)
    theirs = lax.ppermute(mine, BOTH, SWAP)
    code_part = plane.astype(F32).sum(0)
    return back.reshape(features.shape), joined(info, mine, theirs), code_part


def solution(mesh):
    in_specs = (
        P("clip", "tile", None, None),
        P(),
        P(),
        P(None, "clip", "tile", None),
        P("clip", "tile", None, None),
    )
    out_specs = (P("clip", "tile", None, None), P(), P(BOTH, None))
    return jax.shard_map(
        on_device, mesh=mesh, in_specs=in_specs, out_specs=out_specs, check_vma=False
    )
```

```python
import functools

import jax
import jax.numpy as jnp
from jax import lax
from jax.experimental import pallas as pl
from jax.experimental.pallas import tpu as pltpu
from jax.sharding import PartitionSpec as P

BETA = 0.25
BOTH = ("clip", "tile")
F32, BF16 = jnp.float32, jnp.bfloat16

CHANS = 256
CODES = 16384
DEPTHS = 4
COLS = 128
ROWS = 16
HERE = 2
SPOTS = HERE * ROWS * COLS
BLOCK = 4 * COLS
BLOCKS = SPOTS // BLOCK
TALL = 4
GROUP = TALL * DEPTHS
STRIPS = SPOTS // (TALL * COLS)
GROUPS = DEPTHS * SPOTS // GROUP
SPILL = 64
CHUNKS = 8
UNROLL = 32
PIECES = 96
PIECE = (16, 384)
SHARE = CODES // 128


def lin(x, y, z, core):
    return (((z & 1) * 4 + y) * 2 + core) * 8 + x * 2 + (z >> 1)


def moves(where):
    return [
        (lin(x, y, z, c), lin(*where(x, y, z, c)))
        for x in range(4)
        for y in range(4)
        for z in range(4)
        for c in range(2)
    ]


SWAP = moves(lambda x, y, z, c: (x, y, z, 1 - c))


def first_ring(d):
    return moves(lambda x, y, z, c: ((x + d) % 4, y, z, c) if c == 0 else (x, (y + d) % 4, z, c))


PLANES = [[lin(x, y, z, 0) for y in range(4) for z in range(4)] for x in range(4)] + [
    [lin(x, y, z, 1) for x in range(4) for z in range(4)] for y in range(4)
]


def place():
    clip, tile = lax.axis_index("clip"), lax.axis_index("tile")
    core, y, z_lo = clip % 2, (clip // 2) % 4, clip // 8
    x, z_hi = tile // 2, tile % 2
    return jnp.stack([x, y, z_hi * 2 + z_lo, core, tile, lax.axis_size("tile")]).astype(jnp.int32)


def owner(x0, y0, core, j, m):
    other, z = m >> 2, m & 3
    x = jnp.where(core == 0, (x0 + j) & 3, other)
    y = jnp.where(core == 0, other, (y0 + j) & 3)
    return lin(x, y, z, core)


def shifted(value, by):
    n = value.shape[0]
    col = lax.broadcasted_iota(jnp.int32, value.shape, 0) % COLS
    if by == 1:
        return jnp.where(col == 0, 0.0, pltpu.roll(value, 1, axis=0))
    return jnp.where(col == COLS - 1, 0.0, pltpu.roll(value, n - 1, axis=0))


def window_copies(above, mid, below, window, sems, first=0):
    found = []
    for n in range(HERE):
        for source, row, count in ((above, 0, 1), (mid, 1, ROWS), (below, ROWS + 1, 1)):
            found.append(
                pltpu.make_async_copy(
                    source.at[n], window.at[n, pl.ds(row, count)], sems.at[first + len(found)]
                )
            )
    return found


def list_kernel(codes, marked, extra, parts):
    cells = [
        codes[pl.ds(d * HERE * ROWS + r, STRIPS, stride=TALL), :]
        for r in range(TALL)
        for d in range(DEPTHS)
    ]
    later = []
    for a in range(GROUP):
        hit = None
        for b in range(a + 1, GROUP):
            same = (cells[a] == cells[b]).astype(jnp.int32)
            hit = same if hit is None else jnp.maximum(hit, same)
        later.append(jnp.zeros_like(cells[a]) if hit is None else hit)
    flags = jnp.concatenate(later, axis=0)
    entries = jnp.concatenate(cells, axis=0)
    line = lax.broadcasted_iota(jnp.int32, (128, 128), 0)
    lane = lax.broadcasted_iota(jnp.int32, (128, 128), 1)
    bits = flags.astype(F32)
    inside = jnp.dot(bits, (line < lane).astype(F32), preferred_element_type=F32)
    per_row = jnp.dot(bits, jnp.ones((128, 128), F32), preferred_element_type=F32)
    ahead = jnp.dot((lane < line).astype(F32), per_row, preferred_element_type=F32)
    rank = (inside + ahead).astype(jnp.int32)
    marked[...] = 2 * jnp.where(flags > 0, CODES + rank, entries)
    rank = jnp.where(flags > 0, rank, -1)
    for s in range(SPILL):
        parts[pl.ds(s, 1), :] = jnp.sum(
            jnp.where(rank == s, 2 * entries, 0), axis=0, keepdims=True
        )
    codes_of = jnp.sum(parts[pl.ds(0, SPILL), :].astype(F32), axis=1, keepdims=True)
    square = lax.broadcasted_iota(jnp.int32, (SPILL, 128), 0) == lax.broadcasted_iota(
        jnp.int32, (SPILL, 128), 1
    )
    spilled = jnp.sum(jnp.where(square, codes_of, 0.0), axis=0, keepdims=True)
    whole = jnp.sum(per_row, axis=0, keepdims=True)
    both = jnp.concatenate([jnp.broadcast_to(spilled, (4, 128)), jnp.broadcast_to(whole, (4, 128))])
    extra[...] = both.astype(jnp.int32)


def entry_lists(codes):
    ints = jnp.int32
    return pl.pallas_call(
        list_kernel,
        out_shape=[
            jax.ShapeDtypeStruct((128, 128), ints),
            jax.ShapeDtypeStruct((8, 128), ints),
        ],
        scratch_shapes=[pltpu.VMEM((SPILL + 8, 128), ints)],
    )(codes.reshape(128, 128))


def quantizer_kernel(
    extra, info,
    marked, plain, codebook, feats, above, below, weights, up,
    grad, grad_first, grad_last, send, keep, weight_send, weight_keep,
    table, sums, lat, raw, near, taps, window, weight_sum, weight_out, all_ids, sems, *ids,
):
    many = extra[4, 0]
    windows = window_copies(above, feats, below, window, sems)
    get_taps = pltpu.make_async_copy(weights, taps, sems.at[6])
    get_ids = [
        pltpu.make_async_copy(marked.at[pl.ds(c * GROUPS, GROUPS)], ids[c], sems.at[26 + c])
        for c in range(GROUP)
    ]
    get_up = pltpu.make_async_copy(up, near, sems.at[8])
    chunk = CODES // CHUNKS

    def get_table(c):
        rows = pl.ds(c * chunk, chunk)
        return pltpu.make_async_copy(codebook.at[rows], raw.at[rows], sems.at[16 + c])

    early = [get_taps] + windows[:3]
    for copy in early + windows[3:]:
        copy.start()
    for copy in early + windows[3:]:
        copy.wait()
    close_frame(info, window)
    for c in range(CHUNKS):
        get_table(c).start()
    for copy in get_ids + [get_up]:
        copy.start()

    def line(block, r):
        return pl.multiple_of(block * (2 * TALL * COLS), 8) + 2 * r

    def convolve(block, carry):
        clip = block >> 2
        row = (block & 3) * 4
        cols = [None] * 3
        for a in range(3):
            part = window[clip, pl.ds(row + a, 4)].reshape(BLOCK, CHANS)
            for b in range(3):
                term = jnp.dot(part, taps[3 * a + b], preferred_element_type=F32)
                cols[b] = term if a == 0 else cols[b] + term
        latent = shifted(cols[0], 1) + cols[1] + shifted(cols[2], -1)
        for r in range(4):
            at = line(block, r)
            own = latent[r * COLS : (r + 1) * COLS]
            lat[pl.ds(at, COLS, stride=2 * TALL), :] = own[:, :128]
            lat[pl.ds(at + 1, COLS, stride=2 * TALL), :] = own[:, 128:]
        return carry

    lax.fori_loop(0, BLOCKS, convolve, 0)

    for c in range(CHUNKS):
        get_table(c).wait()

        def convert(t, carry):
            at = pl.multiple_of(c * chunk + t * 512, 16)
            part = raw[pl.ds(at, 512), :].astype(F32)
            at = pl.multiple_of(2 * at, 8)
            table[pl.ds(at, 512, stride=2), :] = part[:, :128]
            table[pl.ds(at + 1, 512, stride=2), :] = part[:, 128:]
            sums[pl.ds(at, 1024), :] = jnp.zeros((1024, 128), F32)
            return carry

        lax.fori_loop(0, chunk // 512, convert, 0)

    sums[pl.ds(2 * CODES, 2 * SPILL), :] = jnp.zeros((2 * SPILL, 128), F32)

    def lend(s, carry):
        table[pl.ds(2 * (CODES + s), 2), :] = table[pl.ds(extra[0, s], 2), :]
        return carry

    lax.fori_loop(0, jnp.minimum(many, SPILL), lend, 0)

    def resids(group, code):
        found = []
        first = pl.multiple_of(group * (2 * TALL), 8)
        for r in range(TALL):
            here = pl.ds(first + 2 * r, 2)
            resid, total = lat[here, :], None
            for d in range(DEPTHS):
                k = code(r, d)
                resid = resid - table[pl.ds(k, 2), :]
                total = resid if total is None else total + resid
                found.append((k, resid))
            lat[here, :] = total
        return found

    for copy in get_ids:
        copy.wait()

    @pl.when(many <= SPILL)
    def _():
        def blocks(block, carry):
            def step(col, carry):
                first = block * COLS + col
                found = resids(first, lambda r, d: ids[r * DEPTHS + d][first])
                new = [sums[pl.ds(k, 2), :] + v for k, v in found]
                for (k, _), v in zip(found, new):
                    sums[pl.ds(k, 2), :] = v
                return carry

            return lax.fori_loop(0, COLS, step, carry, unroll=UNROLL)

        lax.fori_loop(0, STRIPS, blocks, 0)

        def give_back(s, carry):
            k = extra[0, s]
            sums[pl.ds(k, 2), :] = sums[pl.ds(k, 2), :] + sums[pl.ds(2 * (CODES + s), 2), :]
            return carry

        lax.fori_loop(0, many, give_back, 0)

    @pl.when(many > SPILL)
    def _():
        again = pltpu.make_async_copy(plain, all_ids, sems.at[7])
        again.start()
        again.wait()

        def blocks(block, carry):
            def step(col, carry):
                spot = block * (TALL * COLS) + col
                for k, v in resids(block * COLS + col, lambda r, d: 2 * all_ids[d * SPOTS + spot + r * COLS]):
                    sums[pl.ds(k, 2), :] = sums[pl.ds(k, 2), :] + v
                return carry

            return lax.fori_loop(0, COLS, step, carry)

        lax.fori_loop(0, STRIPS, blocks, 0)

    get_up.wait()

    def put_grad(block):
        rows = pl.ds(pl.multiple_of(block * BLOCK, 16), BLOCK)
        return pltpu.make_async_copy(near.at[rows], grad.at[rows], sems.at[8 + block])

    def gradient(block, carry):
        rows = pl.ds(pl.multiple_of(block * BLOCK, 16), BLOCK)
        halves = [
            jnp.concatenate(
                [lat[pl.ds(line(block, r) + h, COLS, stride=2 * TALL), :] for r in range(4)], axis=0
            )
            for h in range(2)
        ]
        total = jnp.concatenate(halves, axis=1)
        near[rows, :] = (near[rows, :].astype(F32) + 2.0 * BETA * total).astype(BF16)
        put_grad(block).start()
        return carry

    lax.fori_loop(0, BLOCKS, gradient, 0)
    put_edges = []
    for out, row in ((grad_first, 0), (grad_last, ROWS - 1)):
        for n in range(HERE):
            rows = pl.ds((n * ROWS + row) * COLS, COLS)
            put_edges.append(
                pltpu.make_async_copy(
                    near.at[rows], out.at[n, 0], sems.at[26 + GROUP + len(put_edges)]
                )
            )
    for copy in put_edges:
        copy.start()

    def put_out(out, first, j):
        rows = pl.ds((first + j) * 16 * SHARE, 16 * SHARE)
        return pltpu.make_async_copy(raw.at[rows], out.at[j], sems.at[16 + first + j])

    def fill(m, carry, first, core, j):
        at = pl.multiple_of(owner(info[0], info[1], core, j, m) * (2 * SHARE), 8)
        rows = pl.ds(pl.multiple_of(((first + j) * 16 + m) * SHARE, 16), SHARE)
        raw[rows, :128] = (sums[pl.ds(at, SHARE, stride=2), :] * -2.0).astype(BF16)
        raw[rows, 128:] = (sums[pl.ds(at + 1, SHARE, stride=2), :] * -2.0).astype(BF16)
        return carry

    for first, core, out in ((0, 1 - info[3], send), (4, info[3], keep)):
        for j in range(4):
            lax.fori_loop(0, 16, functools.partial(fill, first=first, core=core, j=j), 0, unroll=4)
            put_out(out, first, j).start()

    weight_sum[...] = jnp.zeros_like(weight_sum)

    def weigh(block, carry):
        clip = block // (ROWS // 4)
        row = (block % (ROWS // 4)) * 4
        own = near[pl.ds(pl.multiple_of(block * BLOCK, 16), BLOCK), :]
        mid = own.astype(F32)
        wide = jnp.concatenate(
            [shifted(mid, -1).astype(BF16), own, shifted(mid, 1).astype(BF16)], axis=1
        )
        for a in range(3):
            part = window[clip, pl.ds(row + a, 4)].reshape(BLOCK, CHANS)
            weight_sum[pl.ds(a * CHANS, CHANS), :] += lax.dot_general(
                part, wide, (((0,), (0,)), ((), ())), preferred_element_type=F32
            )
        return carry

    lax.fori_loop(0, BLOCKS, weigh, 0)

    def cut(side, core, j):
        ring = (jnp.where(core == 0, info[0], info[1]) + j) % 4
        first = pl.multiple_of(jnp.minimum(core * 64 + ring * 16, PIECES - 16) * 8, 128)
        for m in range(16):
            rows = weight_sum[pl.ds(first + 8 * m, 8), :]
            both = jnp.concatenate([rows[:, :384], rows[:, 384:]], axis=0)
            weight_out[side, j, m] = both.astype(BF16)

    def put_weights(out, side):
        return pltpu.make_async_copy(weight_out.at[side], out, sems.at[24 + side])

    for side, core, out in ((0, 1 - info[3], weight_send), (1, info[3], weight_keep)):
        for j in range(4):
            cut(side, core, j)
        put_weights(out, side).start()
    for copy in put_edges:
        copy.wait()
    for block in range(BLOCKS):
        put_grad(block).wait()
    for first, out in ((0, send), (4, keep)):
        for j in range(4):
            put_out(out, first, j).wait()
    put_weights(weight_send, 0).wait()
    put_weights(weight_keep, 1).wait()


def quantizer(marked, plain, extra, info, codebook, feats, above, below, weights, up):
    hbm = pl.BlockSpec(memory_space=pl.ANY)
    smem = pl.BlockSpec(memory_space=pltpu.SMEM)
    vmem = pl.BlockSpec(memory_space=pltpu.VMEM)
    out_shape = (4, 16 * SHARE, CHANS)
    weight_shape = (4, 16) + PIECE
    return pl.pallas_call(
        quantizer_kernel,
        in_specs=[smem] * 2 + [hbm] * 4 + [vmem] * 2 + [hbm] * 2,
        out_specs=[hbm] * 7,
        scratch_shapes=[
            pltpu.VMEM((2 * (CODES + SPILL) + 8, 128), F32),
            pltpu.VMEM((2 * (CODES + SPILL) + 8, 128), F32),
            pltpu.VMEM((2 * SPOTS + 8, 128), F32),
            pltpu.VMEM((CODES, CHANS), BF16),
            pltpu.VMEM((SPOTS, CHANS), BF16),
            pltpu.VMEM((9, CHANS, CHANS), BF16),
            pltpu.VMEM((HERE, ROWS + 2, COLS, CHANS), BF16),
            pltpu.VMEM((3 * CHANS, 3 * CHANS), F32),
            pltpu.VMEM((2,) + weight_shape, BF16),
            pltpu.SMEM((DEPTHS * SPOTS,), jnp.int32),
            pltpu.SemaphoreType.DMA((26 + GROUP + 2 * HERE,)),
        ]
        + [pltpu.SMEM((GROUPS,), jnp.int32)] * GROUP,
        out_shape=[
            jax.ShapeDtypeStruct((SPOTS, CHANS), BF16),
            jax.ShapeDtypeStruct((HERE, 1, COLS, CHANS), BF16),
            jax.ShapeDtypeStruct((HERE, 1, COLS, CHANS), BF16),
            jax.ShapeDtypeStruct(out_shape, BF16),
            jax.ShapeDtypeStruct(out_shape, BF16),
            jax.ShapeDtypeStruct(weight_shape, BF16),
            jax.ShapeDtypeStruct(weight_shape, BF16),
        ],
        compiler_params=pltpu.CompilerParams(vmem_limit_bytes=58 << 20),
        cost_estimate=pl.CostEstimate(
            flops=4 * 9 * SPOTS * CHANS * CHANS, bytes_accessed=64 << 20, transcendentals=0
        ),
    )(extra, info, marked, plain, codebook, feats, above, below, weights, up)


def back_kernel(info, grad, above, below, weights, out, window, sems):
    i = pl.program_id(0)

    copies = window_copies(above, grad, below, window, sems)

    @pl.when(i == 0)
    def _():
        for copy in copies:
            copy.start()
        for copy in copies:
            copy.wait()
        close_frame(info, window)

    clip = i // (ROWS // 4)
    row = (i % (ROWS // 4)) * 4
    cols = [None] * 3
    for a in range(3):
        part = window[clip, pl.ds(row + 2 - a, 4)].reshape(BLOCK, CHANS)
        for b in range(3):
            term = lax.dot_general(
                part, weights[3 * a + b], (((1,), (1,)), ((), ())), preferred_element_type=F32
            )
            cols[b] = term if a == 0 else cols[b] + term
    back = shifted(cols[0], -1) + cols[1] + shifted(cols[2], 1)
    out[...] = back.astype(BF16)


def feature_grads(info, grad, above, below, weights):
    return pl.pallas_call(
        back_kernel,
        grid=(BLOCKS,),
        in_specs=[
            pl.BlockSpec(memory_space=pltpu.SMEM),
            pl.BlockSpec(memory_space=pl.ANY),
            pl.BlockSpec(memory_space=pl.ANY),
            pl.BlockSpec(memory_space=pl.ANY),
            pl.BlockSpec((9, CHANS, CHANS), lambda i: (0, 0, 0)),
        ],
        out_specs=pl.BlockSpec((BLOCK, CHANS), lambda i: (i, 0)),
        scratch_shapes=[
            pltpu.VMEM((HERE, ROWS + 2, COLS, CHANS), BF16),
            pltpu.SemaphoreType.DMA((3 * HERE,)),
        ],
        out_shape=jax.ShapeDtypeStruct((SPOTS, CHANS), BF16),
        compiler_params=pltpu.CompilerParams(
            vmem_limit_bytes=32 << 20, dimension_semantics=("arbitrary",)
        ),
        cost_estimate=pl.CostEstimate(
            flops=2 * 9 * SPOTS * CHANS * CHANS, bytes_accessed=8 << 20, transcendentals=0
        ),
    )(info, grad, above, below, weights)


def add_kernel(*refs):
    *parts, out = refs
    rows = 256

    def add(i, carry):
        here = pl.ds(pl.multiple_of(i * rows, 16), rows)
        total = parts[0][here, :].astype(F32)
        for part in parts[1:]:
            total = total + part[here, :].astype(F32)
        out[here, :] = total.astype(BF16)
        return carry

    lax.fori_loop(0, out.shape[0] // rows, add, 0)


def added(*parts):
    shape = parts[0].shape
    flat = [part.reshape(-1, CHANS) for part in parts]
    total = pl.pallas_call(
        add_kernel,
        out_shape=jax.ShapeDtypeStruct(flat[0].shape, BF16),
        compiler_params=pltpu.CompilerParams(vmem_limit_bytes=24 << 20),
        cost_estimate=pl.CostEstimate(
            flops=2 * flat[0].size, bytes_accessed=8 * flat[0].size, transcendentals=0
        ),
    )(*flat)
    return total.reshape(shape)


def turn_kernel(info, *refs):
    at = jnp.where(info[3] == 0, info[0], info[1])
    for d in range(4):
        refs[4][(at + 4 - d) % 4] = refs[d][...]


def turned(info, pieces, around):
    return pl.pallas_call(
        turn_kernel,
        in_specs=[pl.BlockSpec(memory_space=pltpu.SMEM)] + [pl.BlockSpec()] * 4,
        out_shape=jax.ShapeDtypeStruct((4,) + pieces.shape, BF16),
    )(info, pieces, *around)


def join_kernel(info, mine, theirs, out):
    def join(low, high):
        for a in range(3):
            for r in range(2):

                def place(m, carry):
                    ref, ring = (low, 2 * a + r) if a < 2 else (high, r)
                    both = ref[ring, m].astype(F32)
                    top, bottom = both[:8], both[8:]
                    rows = pl.ds(pl.multiple_of((r * 16 + m) * 8, 8), 8)
                    out[3 * a, rows, :] = top[:, :256]
                    out[3 * a + 1, rows, :128] = top[:, 256:]
                    out[3 * a + 1, rows, 128:] = bottom[:, :128]
                    out[3 * a + 2, rows, :] = bottom[:, 128:]
                    return carry

                lax.fori_loop(0, 16, place, 0, unroll=4)

    @pl.when(info[3] == 0)
    def _():
        join(mine, theirs)

    @pl.when(info[3] != 0)
    def _():
        join(theirs, mine)


def joined(info, mine, theirs):
    return pl.pallas_call(
        join_kernel,
        in_specs=[pl.BlockSpec(memory_space=pltpu.SMEM)] + [pl.BlockSpec()] * 2,
        out_shape=jax.ShapeDtypeStruct((9, CHANS, CHANS), F32),
        compiler_params=pltpu.CompilerParams(vmem_limit_bytes=32 << 20),
    )(info, mine, theirs)


def edges(first, last):
    n = lax.axis_size("tile")
    above = lax.ppermute(last, "tile", [(i, (i + 1) % n) for i in range(n)])
    below = lax.ppermute(first, "tile", [((i + 1) % n, i) for i in range(n)])
    return above, below


def close_frame(info, window):
    @pl.when(info[4] == 0)
    def _():
        window[:, 0] = jnp.zeros((HERE, COLS, CHANS), BF16)

    @pl.when(info[4] == info[5] - 1)
    def _():
        window[:, ROWS + 1] = jnp.zeros((HERE, COLS, CHANS), BF16)


def on_device(features, conv_weight, codebook, codes, upstream):
    info = place()
    above, below = edges(features[:, :1], features[:, -1:])
    marked, extra = entry_lists(codes)
    grad, grad_first, grad_last, send, keep, weight_send, weight_keep = quantizer(
        marked.reshape(-1), codes.reshape(-1), extra, info, codebook, features, above, below,
        conv_weight, upstream.reshape(SPOTS, CHANS),
    )
    got = lax.ppermute(send, BOTH, SWAP)
    grad4 = grad.reshape(features.shape)
    grad_above, grad_below = edges(grad_first, grad_last)
    weight_got = lax.ppermute(weight_send, BOTH, SWAP)
    weight_chip = (weight_keep.astype(F32) + weight_got.astype(F32)).astype(BF16)
    keep, got, grad_above, grad_below = lax.optimization_barrier(
        (keep, got, grad_above, grad_below)
    )
    weight_ring = weight_chip[0].astype(F32)
    for d in (1, 2, 3):
        weight_ring = weight_ring + lax.ppermute(weight_chip[d], BOTH, first_ring(d)).astype(F32)
    chip = [
        (keep[j].astype(F32) + got[j].astype(F32)).astype(BF16).reshape(16, SHARE, CHANS)
        for j in range(4)
    ]
    others = [lax.ppermute(chip[d], BOTH, first_ring(d)) for d in (1, 2, 3)]
    weight_ring, grad_above = lax.optimization_barrier((weight_ring.astype(BF16), grad_above))
    plane = lax.all_to_all(weight_ring, BOTH, 0, 0, axis_index_groups=PLANES)
    back = feature_grads(info, grad4, grad_above, grad_below, conv_weight)
    piece = plane.astype(F32).sum(0).astype(BF16)
    piece, back = lax.optimization_barrier((piece, back))
    pieces = lax.all_to_all(
        jnp.broadcast_to(piece[None], (16,) + PIECE), BOTH, 0, 0, axis_index_groups=PLANES
    )
    ring = added(chip[0], *others)
    pieces, ring = lax.optimization_barrier((pieces, ring))
    plane = lax.all_to_all(ring, BOTH, 0, 0, axis_index_groups=PLANES)
    around = [lax.ppermute(pieces, BOTH, first_ring(d)) for d in (1, 2, 3)]
    mine = turned(info, pieces, around)
    theirs = lax.ppermute(mine, BOTH, SWAP)
    code_part = plane.astype(F32).sum(0)
    return back.reshape(features.shape), joined(info, mine, theirs), code_part


def solution(mesh):
    in_specs = (
        P("clip", "tile", None, None),
        P(),
        P(),
        P(None, "clip", "tile", None),
        P("clip", "tile", None, None),
    )
    out_specs = (P("clip", "tile", None, None), P(), P(BOTH, None))
    return jax.shard_map(
        on_device, mesh=mesh, in_specs=in_specs, out_specs=out_specs, check_vma=False
    )
```
